256 devices in a mesh: slab: 4 (over x), row: 8 (over y, z_hi), col: 8 (over z_lo, core).
Axes of the slice: x: 4, y: 4, z: 8 (z_hi: 2, z_lo: 4; z = z_hi * 4 + z_lo), core: 2. Of those that a mesh axis runs over, the one named last changes fastest.
Arguments:
- wave: float32 [16, 32, 64, 1024], P(None, 'slab', 'row', 'col')
- potential: float32 [32, 64, 1024], P('slab', 'row', 'col'), may hold values from -1 to 1
- positions: int32 [3, 2048], P(None, ('slab', 'row', 'col')), may hold values from 0 to 1023, as said below
- species: int32 [2048], P(('slab', 'row', 'col')), may hold values from 0 to 3
- counts: int32 [256], P(('slab', 'row', 'col')), may hold values from 1 to 8, as said below
- offsets: int32 [4, 3, 384], replicated, may hold values from -5 to 5, as said below
- beta: float32 [4, 384], replicated, may hold values from -0.3125 to 0.3125
- coupling: float32 [4], replicated, may hold values from 0.5 to 4
Outputs:
- filtered: float32 [16, 32, 64, 1024], P(None, 'slab', 'row', 'col')
- gram: float32 [16, 16], replicated
The draws below stay inside these ranges and needn't reach their ends.
Inputs may be any that keep to these rules, and one draw needn't show every extreme that they name: `positions`: slot j belongs to block j // 8, blocks numbered with the first dimension slowest and the third fastest; its position lies inside that block of 8 x 8 x 128 cells; the first slot sits at the grid's first cell and the last slot at its last cell. `counts`: some block has all 8 slots live. `offsets`: each species' points are distinct lattice points at distance 5 or less from the anchor, and include the six points at distance 5 along the axes.
All inputs are finite; a program needn't handle non-finite values.
Results may differ from the reference program's by a relative error of at most 0.000086.
Values sent between devices are 32-bit elements; how exact they have to be, the bound alone decides.
No kernel may reach another device: no remote copies, remote signals or barrier semaphores. Data moves between devices by JAX's collectives and lax.ppermute only.
A program may use at most 192 MiB of HBM per device.

```python
import math
import jax
import jax.numpy as jnp
import numpy as np
from jax import lax

BANDS = 16
SPECIES = 4
POINTS = 384
CX = 8
CY = 8
CZ = 128
ACAP = 8
NX = 32
NY = 64
NZ = 1024
ATOMS = 2048


ball_reach = 5


def ball_table():
    axis_points = []
    other_points = []
    for step_x in range(-ball_reach, ball_reach + 1):
        for step_y in range(-ball_reach, ball_reach + 1):
            for step_z in range(-ball_reach, ball_reach + 1):
                radius_sq = step_x * step_x + step_y * step_y + step_z * step_z
                if radius_sq <= ball_reach * ball_reach:
                    if radius_sq == ball_reach * ball_reach and (abs(step_x) == ball_reach or abs(step_y) == ball_reach or abs(step_z) == ball_reach):
                        axis_points.append((step_x, step_y, step_z))
                    else:
                        other_points.append((step_x, step_y, step_z))
    return np.array(axis_points + other_points, dtype=np.int32)


def draw_wave(key, part):
    key = jax.random.fold_in(key, 11)
    noise_key = jax.random.fold_in(key, 0)
    noise = jax.random.normal(noise_key, (BANDS, NX, NY, NZ), jnp.float32)
    depth = jnp.arange(NX, dtype=jnp.float32) / (NX - 1)
    envelope = (1.0 + 2.0 * depth)[None, :, None, None]
    return noise * envelope


def draw_positions(key, part):
    key = jax.random.fold_in(key, 12)
    blocks = NX // CX * (NY // CY) * (NZ // CZ)
    total = ACAP * blocks
    slots = jnp.arange(total, dtype=jnp.int32)
    owner = slots // ACAP
    columns = NZ // CZ
    rows = NY // CY
    block_x = owner // (rows * columns)
    block_y = owner // columns % rows
    block_z = owner % columns
    key_x, key_y, key_z = jax.random.split(key, 3)
    place_x = block_x * CX + jax.random.randint(key_x, (total,), 0, CX)
    place_y = block_y * CY + jax.random.randint(key_y, (total,), 0, CY)
    place_z = block_z * CZ + jax.random.randint(key_z, (total,), 0, CZ)
    placed = jnp.stack([place_x, place_y, place_z]).astype(jnp.int32)
    placed = placed.at[:, 0].set(jnp.zeros((3,), jnp.int32))
    placed = placed.at[:, total - 1].set(jnp.array([NX - 1, NY - 1, NZ - 1], dtype=jnp.int32))
    return placed.astype(jnp.int32)


def draw_counts(key, part):
    key = jax.random.fold_in(key, 13)
    blocks = NX // CX * (NY // CY) * (NZ // CZ)
    first_key, second_key = jax.random.split(key)
    drawn = jax.random.randint(first_key, (blocks,), 1, ACAP + 1)
    chosen = jax.random.randint(second_key, (), 0, blocks)
    return drawn.at[chosen].set(ACAP).astype(jnp.int32)


def draw_offsets(key, part):
    key = jax.random.fold_in(key, 14)
    table = jnp.asarray(ball_table())
    remaining = table.shape[0] - 6
    stacked = []
    for kind in range(SPECIES):
        order = jax.random.permutation(jax.random.fold_in(key, kind), remaining)[:POINTS - 6] + 6
        chosen = jnp.concatenate([jnp.arange(6, dtype=jnp.int32), order.astype(jnp.int32)])
        stacked.append(table[chosen].T)
    return jnp.stack(stacked).astype(jnp.int32)


def plant(values, own_key, low, top_value):
    index_at = [jax.random.randint(jax.random.fold_in(own_key, axis), (), 0, length) for axis, length in enumerate(values.shape)]
    main_axis = values.shape.index(max(values.shape))
    next_to = index_at[:main_axis] + [(index_at[main_axis] + 1) % values.shape[main_axis]] + index_at[main_axis + 1:]
    return values.at[tuple(index_at)].set(low).at[tuple(next_to)].set(top_value)


def levels(own_key, shape, cuts, low, top_value):
    loudness = 1.0
    for position, parts in cuts:
        draws = jax.random.uniform(jax.random.fold_in(jax.random.fold_in(own_key, 6), position), (parts,), jnp.float32, low / len(cuts), top_value / len(cuts))
        loudness = loudness * jnp.repeat(jnp.exp(draws), shape[position] // parts).reshape((-1,) + (1,) * (len(shape) - 1 - position))
    return loudness


def bell_draw(own_key, shape, scale, most, kind=jnp.bfloat16):
    values = scale * jax.random.normal(own_key, shape, jnp.float32)
    return jnp.clip(values, min=-most, max=most).astype(kind)


def setup_inputs(seed: int = 0) -> dict:
    streams_of = jax.random.split(jax.random.key(seed), 9)
    return {
        "wave": draw_wave(jax.random.fold_in(streams_of[8], 71), 0),
        "potential": jnp.clip(jax.random.uniform(streams_of[1], (NX, NY, NZ), jnp.float32, -1.0, 1.0) * levels(streams_of[1], (NX, NY, NZ), ((0, 4), (1, 8), (2, 8)), -0.4, 0.0), -1.0, 1.0),
        "positions": draw_positions(jax.random.fold_in(streams_of[8], 71), 0),
        "species": plant(jax.random.randint(streams_of[3], (ATOMS,), 0, SPECIES), jax.random.fold_in(streams_of[3], 1), 0, SPECIES - 1).astype(jnp.int32),
        "counts": draw_counts(jax.random.fold_in(streams_of[8], 71), 0),
        "offsets": draw_offsets(jax.random.fold_in(streams_of[8], 71), 0),
        "beta": bell_draw(streams_of[6], (SPECIES, POINTS), POINTS ** -0.5, 0.3125, jnp.float32),
        "coupling": jnp.clip(jnp.exp(jax.random.uniform(streams_of[7], (SPECIES,), jnp.float32, math.log(0.5), math.log(4.0))), 0.5, 4.0),
    }


stencil_weights = (-5369.0 / 1800.0, 12.0 / 7.0, -15.0 / 56.0, 10.0 / 189.0, -1.0 / 112.0, 2.0 / 1925.0, -1.0 / 16632.0)
lower_edge = 3.0
upper_edge = 17.0


def stencil(padded, extent):
    size_x, size_y, size_z = extent

    def window(shift_x, shift_y, shift_z):
        return padded[:, 6 + shift_x:6 + shift_x + size_x, 6 + shift_y:6 + shift_y + size_y, 6 + shift_z:6 + shift_z + size_z]

    total = (3.0 * stencil_weights[0]) * window(0, 0, 0)
    for reach in range(1, 7):
        paired = window(reach, 0, 0) + window(-reach, 0, 0) + window(0, reach, 0) + window(0, -reach, 0) + window(0, 0, reach) + window(0, 0, -reach)
        total = total + stencil_weights[reach] * paired
    return total


def nonlocal_term(field, positions, species, counts, offsets, beta, coupling):
    bands = field.shape[0]
    atoms = positions.shape[1]
    slots = jnp.arange(atoms, dtype=jnp.int32)
    active = (slots % ACAP < counts[slots // ACAP]).astype(jnp.float32)
    points = positions.T[:, :, None] + offsets[species]
    limits = jnp.array([NX, NY, NZ], dtype=jnp.int32)[None, :, None]
    inside = jnp.all((points >= 0) & (points < limits), axis=1)
    flat_index = (points[:, 0] * NY + points[:, 1]) * NZ + points[:, 2]
    flat_index = jnp.where(inside, flat_index, NX * NY * NZ).astype(jnp.int32).reshape(-1)
    values = field.reshape(bands, -1)
    picked = jnp.take(values, flat_index, axis=1, mode="fill", fill_value=0.0).reshape(bands, atoms, -1)
    shapes = beta[species]
    projected = jnp.sum(picked * shapes[None], axis=2)
    scaled = projected * (coupling[species] * active)[None]
    spread = (scaled[:, :, None] * shapes[None]).reshape(bands, -1)
    result = jnp.zeros_like(values).at[:, flat_index].add(spread, mode="drop")
    return result.reshape(field.shape)


def reference(wave, potential, positions, species, counts, offsets, beta, coupling):
    centre = 0.5 * (upper_edge + lower_edge)
    half_width = 0.5 * (upper_edge - lower_edge)

    def filter_step(field):
        padded = jnp.pad(field, ((0, 0), (6, 6), (6, 6), (6, 6)))
        applied = -0.5 * stencil(padded, field.shape[1:]) + potential[None] * field
        applied = applied + nonlocal_term(field, positions, species, counts, offsets, beta, coupling)
        return (applied - centre * field) / half_width

    first = filter_step(wave)
    second = 2.0 * filter_step(first) - wave
    third = 2.0 * filter_step(second) - first
    flattened = third.reshape(third.shape[0], -1)
    gram = jnp.dot(flattened, flattened.T, precision=lax.Precision.HIGHEST) / (NX * NY * NZ)
    return third, gram
```

```python
import jax
import jax.numpy as jnp
from jax import lax
from jax.experimental import pallas as pl
from jax.experimental.pallas import tpu as pltpu
from jax.sharding import PartitionSpec as P

stencil_weights = (
    -5369.0 / 1800.0,
    12.0 / 7.0,
    -15.0 / 56.0,
    10.0 / 189.0,
    -1.0 / 112.0,
    2.0 / 1925.0,
    -1.0 / 16632.0,
)
lower_edge = 3.0
upper_edge = 17.0
centre = 0.5 * (upper_edge + lower_edge)
half_width = 0.5 * (upper_edge - lower_edge)

BANDS = 16
GX, GY, LANES = 32, 64, 128
PX, PY = 6, 8
PITCH = GY + 2 * PY
ROWS = (GX + 2 * PX) * PITCH
TILES = 12
BLOCKS = 32
SLOTS = 8
CAP = 2 * BLOCKS * SLOTS
HALO_ROWS = BLOCKS * 4 * 8 + BLOCKS
FAR = -4096
VMEM = pl.BlockSpec(memory_space=pltpu.VMEM)
SMEM = pl.BlockSpec(memory_space=pltpu.SMEM)
HIGHEST = lax.Precision.HIGHEST


def lane_of(shape):
    return lax.broadcasted_iota(jnp.int32, shape, len(shape) - 1)


def row_of(shape):
    return lax.broadcasted_iota(jnp.int32, shape, len(shape) - 2)


def pack_kernel(place, positions, species, counts, wave, potential, out):
    col = place[2]
    low = lane_of((8, LANES)) < 64
    lane = lane_of((8, LANES))
    info = jnp.zeros((8, LANES), jnp.int32)
    for slot in range(SLOTS):
        live = slot < counts[0]
        base = (positions[0, slot] + PX) * PITCH + positions[1, slot] + PY
        z = jnp.where(live, positions[2, slot], FAR)
        info = jnp.where(lane == slot, z, info)
        info = jnp.where(lane == SLOTS + slot, base * 4 + species[slot], info)
    info = info.astype(jnp.float32)

    def halves(tile, other):
        return (
            jnp.where(low, tile, pltpu.roll(other, 64, 1)),
            jnp.where(low, pltpu.roll(tile, 64, 1), other),
        )

    fixed = [halves(potential[k], potential[k + 4]) for k in range(4)]
    for pair in range(2):
        slabs = [lax.rem(2 * pair + h + col, 4) for h in range(2)]

        def one(r, carry):
            band = pair * 8 + r
            for k in range(4):
                parts = halves(wave[band, k], wave[band, k + 4])
                for h in range(2):
                    dest = slabs[h] * 8 + r
                    out[dest, k] = parts[h]
                    out[dest, 4 + k] = fixed[k][h]
            for h in range(2):
                out[slabs[h] * 8 + r, 8] = info
            return carry

        lax.fori_loop(0, 8, one, 0)


def edge_kernel(held, low_out, high_out):
    even = (lane_of((8, LANES)) & 32) == 0

    def one(d, carry):
        for field in range(2):
            for pair in range(2):
                first = held[d, field * 4 + 2 * pair]
                second = held[d, field * 4 + 2 * pair + 1]
                at = pl.multiple_of(d * 32, 32) + field * 16 + pair * 8
                low_out[pl.ds(at, 8), :] = jnp.where(even, first, pltpu.roll(second, 32, 1))
                high_out[pl.ds(at, 8), :] = jnp.where(even, pltpu.roll(first, 96, 1), second)
        return carry

    lax.fori_loop(0, BLOCKS, one, 0)
    rows = held[:, 8, 0, :]
    low_out[BLOCKS * 32 :, :] = rows
    high_out[BLOCKS * 32 :, :] = rows


def sphere_kernel(offsets, beta, out):
    points = beta.shape[1]
    for kind in range(beta.shape[0]):
        dx = offsets[3 * kind : 3 * kind + 1, :]
        dy = offsets[3 * kind + 1 : 3 * kind + 2, :]
        dz = offsets[3 * kind + 2 : 3 * kind + 3, :]
        row = 16 + (dx + 3) * 8 + dy + 4
        row = jnp.where(jnp.abs(dx) == 4, jnp.where(dx > 0, 8, 0) + dy + 3, row)
        row = jnp.where(dy == 4, 72 + dx + 3, row)
        row = jnp.where(jnp.abs(dy) == 5, jnp.where(dy > 0, 81, 80), row)
        row = jnp.where(jnp.abs(dx) == 5, jnp.where(dx > 0, 89, 88), row)
        left = (row_of((TILES * 8, points)) == row).astype(jnp.float32)
        right = jnp.where(row_of((LANES, points)) == dz + 5, beta[kind : kind + 1, :], 0.0)
        out[kind] = lax.dot_general(
            left,
            right,
            (((1,), (1,)), ((), ())),
            precision=HIGHEST,
            preferred_element_type=jnp.float32,
        )


def tile_refs(ref, base):
    yield ref.at[pl.ds(base - 4 * PITCH - 3, 8), :]
    yield ref.at[pl.ds(base + 4 * PITCH - 3, 8), :]
    for dx in range(-3, 4):
        yield ref.at[pl.ds(base + dx * PITCH - 4, 8), :]
    yield ref.at[pl.ds(base - 3 * PITCH + 4, 8, stride=PITCH), :]
    yield ref.at[pl.ds(base - 5, 2, stride=10), :]
    yield ref.at[pl.ds(base - 5 * PITCH, 2, stride=10 * PITCH), :]


TILE_ROWS = (8,) * 10 + (2, 2)


def filter_kernel(
    place,
    coupling,
    held,
    low_in,
    high_in,
    sphere,
    out,
    buf_a,
    buf_b,
    pot,
    zpart,
    rolled,
    acc,
    total,
    table_v,
    table,
    listed,
    extra,
    sem,
):
    slab, col = place[0], place[2]
    half = lax.rem(slab + 4 - lax.rem(col, 4), 4) % 2
    depth = col * 2 + half
    lane8 = lane_of((8, LANES))

    own = held[:, 8, 0, :]
    outer = jnp.where(half == 0, low_in[BLOCKS * 32 :, :], high_in[BLOCKS * 32 :, :])
    rows = jnp.concatenate([own, outer], axis=0).astype(jnp.int32)
    moved = pltpu.roll(rows, LANES - SLOTS, 1)
    lane_z = rows - (depth * 64 - 32)
    kind = jnp.where((lane_z >= 7) & (lane_z < 121), 1, 0)
    kind = kind + jnp.where((lane_z >= 17) & (lane_z < 111), 1, 0)
    kind = kind + jnp.where((lane_z >= 27) & (lane_z < 101), 1, 0)
    kind = jnp.where(moved > 0, kind, 0)
    table_v[...] = jnp.where(kind > 0, moved * 512 + lane_z * 4 + kind, 0)
    copy = pltpu.make_async_copy(table_v, table, sem)
    copy.start()

    buf_a[...] = jnp.zeros_like(buf_a)
    buf_b[...] = jnp.zeros_like(buf_b)
    inner = (lane8 >= 32) & (lane8 < 96)

    def gather_block(d, carry):
        s, r = d // 8, lax.rem(d, 8)
        for x in range(8):
            high, k = x // 4, x % 4
            pair, m = k // 2, k % 2
            group = high * 2 + m
            for field in range(2):
                at = pl.multiple_of(d * 32, 32) + field * 16 + pair * 8
                mid = held[d, field * 4 + k]
                mid = pltpu.roll(mid, (32 - 64 * high) % LANES, 1)
                left = low_in[pl.ds(at, 8), :]
                right = high_in[pl.ds(at, 8), :]
                if group:
                    left = pltpu.roll(left, LANES - 32 * group, 1)
                if group != 3:
                    right = pltpu.roll(right, 96 - 32 * group, 1)
                tile = jnp.where(inner, mid, jnp.where(lane8 < 32, left, right))
                if field == 0:
                    at = pl.multiple_of((s * 8 + x + PX) * PITCH + PY + r * 8, 8)
                    buf_a[pl.ds(at, 8), :] = tile
                else:
                    at = pl.multiple_of((s * 8 + x) * GY + r * 8, 8)
                    pot[pl.ds(at, 8), :] = tile - centre
        return carry

    lax.fori_loop(0, BLOCKS, gather_block, 0)
    copy.wait()

    def sort_slot(i, carry):
        n3, n2, n1 = carry
        for slot in range(SLOTS):
            word = table[i, slot]
            kind = word & 3
            listed[n3] = word
            extra[n2] = word
            extra[CAP + n1] = word
            n3 = n3 + jnp.where(kind == 3, 1, 0)
            n2 = n2 + jnp.where(kind == 2, 1, 0)
            n1 = n1 + jnp.where(kind == 1, 1, 0)
        return n3, n2, n1

    zero = jnp.int32(0)
    n3, n2, n1 = lax.fori_loop(0, 2 * BLOCKS, sort_slot, (zero, zero, zero))

    def move_second(i, carry):
        listed[n3 + i] = extra[i]
        return carry

    def move_first(i, carry):
        listed[n3 + n2 + i] = extra[CAP + i]
        return carry

    lax.fori_loop(0, n2, move_second, 0)
    lax.fori_loop(0, n1, move_first, 0)

    apart = jnp.abs(lane_of((LANES, LANES)) - row_of((LANES, LANES)))
    band = jnp.zeros((LANES, LANES), jnp.float32)
    for reach in range(7):
        band = jnp.where(apart == reach, -0.5 * stencil_weights[reach], band)
    band_high = band.astype(jnp.bfloat16)
    band_low = (band - band_high.astype(jnp.float32)).astype(jnp.bfloat16)

    lanes = lane_of((1, LANES))
    inside = ((lanes >= 32) | (depth > 0)) & ((lanes < 96) | (depth < 15))
    mask = jnp.where(inside, 1.0, 0.0)

    def z_block(source):
        def one(x, carry):
            at = pl.multiple_of((x + PX) * PITCH + PY, 8)
            field = source[pl.ds(at, GY), :]
            high = field.astype(jnp.bfloat16)
            low = (field - high.astype(jnp.float32)).astype(jnp.bfloat16)
            part = jnp.dot(high, band_high, preferred_element_type=jnp.float32)
            part += jnp.dot(low, band_high, preferred_element_type=jnp.float32)
            part += jnp.dot(high, band_low, preferred_element_type=jnp.float32)
            zpart[pl.ds(pl.multiple_of(x * GY, GY), GY), :] = part
            return carry

        lax.fori_loop(0, GX, one, 0)

    def local_part(source, target, scale, subtract):
        z_block(source)
        cube = source.reshape(GX + 2 * PX, PITCH, LANES)

        def one(x, carry):
            at = pl.multiple_of((x + PX) * PITCH + PY, 8)
            own_at = pl.multiple_of(x * GY, GY)
            field = source[pl.ds(at, GY), :]
            result = zpart[pl.ds(own_at, GY), :] + pot[pl.ds(own_at, GY), :] * field
            result += (-1.0 * stencil_weights[0]) * field
            for reach in range(1, 7):
                near = cube[x + PX, pl.ds(PY - reach, GY), :] + cube[x + PX, pl.ds(PY + reach, GY), :]
                near += source[pl.ds(at - reach * PITCH, GY), :]
                near += source[pl.ds(at + reach * PITCH, GY), :]
                result += (-0.5 * stencil_weights[reach]) * near
            result = result * scale
            if subtract:
                result -= target[pl.ds(at, GY), :]
            target[pl.ds(at, GY), :] = result
            return carry

        lax.fori_loop(0, GX, one, 0)

    def gather_atoms(source, count, first):
        def one(j, carry):
            word = listed[j]
            base = word >> 11
            kind = (word >> 9) & 3
            shift = ((word >> 2) & 127) - 5
            weight = coupling[kind]
            parts = []
            small = []
            for t, ref in enumerate(tile_refs(source, base)):
                size = TILE_ROWS[t]
                if first:
                    shape = sphere[kind, 8 * t : 8 * t + size, :]
                    shape = pltpu.roll(shape, shift, 1)
                    rolled[j, 8 * t : 8 * t + size, :] = shape
                else:
                    shape = rolled[j, 8 * t : 8 * t + size, :]
                product = ref[...] * shape
                (parts if size == 8 else small).append(product)
            while len(parts) > 1:
                parts = [a + b for a, b in zip(parts[::2], parts[1::2])] + ([parts[-1]] if len(parts) % 2 else [])
            acc[j] = parts[0] * weight
            acc[j, 0:2, :] += (small[0] + small[1]) * weight
            return carry

        lax.fori_loop(0, count, one, 0)

    def sum_atoms(count, scale):
        def one(i, carry):
            at = pl.multiple_of(i * 32, 32)
            part = jnp.sum(acc[pl.ds(at, 32)], axis=1)
            part = jnp.sum(part, axis=1, keepdims=True) * scale
            total[pl.ds(at, 32), :] = jnp.broadcast_to(part, (32, LANES))
            return carry

        lax.fori_loop(0, (count + 31) // 32, one, 0)

    def spread_atoms(target, count):
        def one(j, carry):
            base = listed[j] >> 11
            q = total[pl.ds(j, 1), :]
            refs = list(tile_refs(target, base))
            values = []
            for t, ref in enumerate(refs):
                size = TILE_ROWS[t]
                values.append(ref[...] + q * rolled[j, 8 * t : 8 * t + size, :])
            for ref, value in zip(refs, values):
                ref[...] = value
            return carry

        lax.fori_loop(0, count, one, 0)

    def clean(target):
        edge = PX * PITCH
        target[0:edge, :] = jnp.zeros((edge, LANES), jnp.float32)
        target[ROWS - edge :, :] = jnp.zeros((edge, LANES), jnp.float32)

        def one(x, carry):
            at = pl.multiple_of((x + PX) * PITCH, 8)
            target[pl.ds(at, PY), :] = jnp.zeros((PY, LANES), jnp.float32)
            target[pl.ds(at + PY + GY, PY), :] = jnp.zeros((PY, LANES), jnp.float32)
            target[pl.ds(at + PY, GY), :] = target[pl.ds(at + PY, GY), :] * mask
            return carry

        lax.fori_loop(0, GX, one, 0)

    def step(source, target, scale, subtract, count, first):
        gather_atoms(source, count, first)
        sum_atoms(count, scale)
        local_part(source, target, scale, subtract)
        spread_atoms(target, count)

    step(buf_a, buf_b, 1.0 / half_width, False, n3 + n2 + n1, True)
    clean(buf_b)
    step(buf_b, buf_a, 2.0 / half_width, True, n3 + n2, False)
    clean(buf_a)
    step(buf_a, buf_b, 2.0 / half_width, True, n3, False)

    low = lane8 < 64

    def send_block(d, carry):
        s, r = d // 8, lax.rem(d, 8)
        for k in range(4):
            at = pl.multiple_of((s * 8 + k + PX) * PITCH + PY + r * 8, 8)
            first = buf_b[pl.ds(at, 8), :]
            second = buf_b[pl.ds(at + 4 * PITCH, 8), :]
            out[d, k] = jnp.where(low, pltpu.roll(first, 96, 1), pltpu.roll(second, 32, 1))
        return carry

    lax.fori_loop(0, BLOCKS, send_block, 0)


def unpack_kernel(place, held, out, gram):
    col = place[2]
    low = lane_of((8, LANES)) < 64
    for pair in range(2):
        slabs = [lax.rem(2 * pair + h + col, 4) for h in range(2)]

        def one(r, carry):
            for k in range(4):
                first = held[slabs[0] * 8 + r, k]
                second = held[slabs[1] * 8 + r, k]
                out[pair * 8 + r, k] = jnp.where(low, first, pltpu.roll(second, 64, 1))
                out[pair * 8 + r, k + 4] = jnp.where(low, pltpu.roll(first, 64, 1), second)
            return carry

        lax.fori_loop(0, 8, one, 0)

    size = BANDS * 8

    def dot(a, b, dims):
        return lax.dot_general(
            a, b, (dims, ((), ())), precision=HIGHEST, preferred_element_type=jnp.float32
        )

    products = jnp.zeros((size, size), jnp.float32)
    for x in range(8):
        plane = out[:, x].reshape(size, LANES)
        products += dot(plane, plane, ((1,), (1,)))
    row, lane = row_of((size, size)), lane_of((size, size))
    products = jnp.where((row & 7) == (lane & 7), products, 0.0)
    pick = (row_of((BANDS, size)) == lane_of((BANDS, size)) // 8).astype(jnp.float32)
    rows = dot(pick, products, ((1,), (0,)))
    spread = (row_of((size, LANES)) // 8 == lane_of((size, LANES))).astype(jnp.float32)
    square = dot(rows, spread, ((1,), (0,)))
    gram[...] = square[0:8] + pltpu.roll(square[8:16], BANDS, 1)


def f32(*shape):
    return jax.ShapeDtypeStruct(shape, jnp.float32)


def params(mib=None):
    return pltpu.CompilerParams(vmem_limit_bytes=None if mib is None else mib << 20)


def shards(wave, potential, positions, species, counts, offsets, beta, coupling):
    place = jnp.stack([lax.axis_index("slab"), lax.axis_index("row"), lax.axis_index("col")])
    packed = pl.pallas_call(
        pack_kernel,
        out_shape=f32(BLOCKS, 9, 8, LANES),
        in_specs=[SMEM, SMEM, SMEM, SMEM, VMEM, VMEM],
        out_specs=VMEM,
        compiler_params=params(16),
        name="pack",
    )(place, positions, species, counts, wave, potential)
    held = lax.all_to_all(packed, ("slab", "row"), split_axis=0, concat_axis=0, tiled=True)

    low_edge, high_edge = pl.pallas_call(
        edge_kernel,
        out_shape=(f32(HALO_ROWS, LANES), f32(HALO_ROWS, LANES)),
        in_specs=[VMEM],
        out_specs=(VMEM, VMEM),
        compiler_params=params(16),
        name="edges",
    )(held)

    order = [((h + 2 * pair + col) % 4) * 8 + col for pair in range(2) for col in range(8) for h in range(2)]
    chains = (order[:16], order[16:])
    up = [(a, b) for chain in chains for a, b in zip(chain[:-1], chain[1:])]
    down = [(b, a) for a, b in up]
    low_in = lax.ppermute(high_edge, ("slab", "col"), up)
    high_in = lax.ppermute(low_edge, ("slab", "col"), down)

    sphere = pl.pallas_call(
        sphere_kernel,
        out_shape=f32(beta.shape[0], TILES * 8, LANES),
        in_specs=[VMEM, VMEM],
        out_specs=VMEM,
        name="sphere",
    )(offsets.reshape(-1, offsets.shape[2]), beta)

    filtered = pl.pallas_call(
        filter_kernel,
        out_shape=f32(BLOCKS, 4, 8, LANES),
        in_specs=[SMEM, SMEM, VMEM, VMEM, VMEM, VMEM],
        out_specs=VMEM,
        scratch_shapes=[
            pltpu.VMEM((ROWS, LANES), jnp.float32),
            pltpu.VMEM((ROWS, LANES), jnp.float32),
            pltpu.VMEM((GX * GY, LANES), jnp.float32),
            pltpu.VMEM((GX * GY, LANES), jnp.float32),
            pltpu.VMEM((CAP, TILES * 8, LANES), jnp.float32),
            pltpu.VMEM((CAP, 8, LANES), jnp.float32),
            pltpu.VMEM((CAP, LANES), jnp.float32),
            pltpu.VMEM((2 * BLOCKS, LANES), jnp.int32),
            pltpu.SMEM((2 * BLOCKS, LANES), jnp.int32),
            pltpu.SMEM((CAP + 1,), jnp.int32),
            pltpu.SMEM((2 * CAP + 1,), jnp.int32),
            pltpu.SemaphoreType.DMA,
        ],
        compiler_params=params(56),
        name="filter",
    )(place, coupling, held, low_in, high_in, sphere)

    back = lax.all_to_all(filtered, ("slab", "row"), split_axis=0, concat_axis=0, tiled=True)
    result, partial = pl.pallas_call(
        unpack_kernel,
        out_shape=(f32(*wave.shape), f32(8, LANES)),
        in_specs=[SMEM, VMEM],
        out_specs=(VMEM, VMEM),
        compiler_params=params(16),
        name="unpack",
    )(place, back)

    def total_over(value, axes, count):
        copies = jnp.broadcast_to(value[None], (count,) + value.shape)
        copies = lax.all_to_all(copies, axes, split_axis=0, concat_axis=0, tiled=True)
        return jnp.sum(copies, axis=0)

    partial = total_over(partial, "col", 8)
    partial = total_over(partial, ("slab", "row"), 32)
    gram = jnp.concatenate([partial[:, :BANDS], partial[:, BANDS : 2 * BANDS]], axis=0)
    cells = 4 * 8 * 8 * 8 * 8 * 128
    return result, gram / cells


def solution(mesh):
    in_specs = (
        P(None, "slab", "row", "col"),
        P("slab", "row", "col"),
        P(None, ("slab", "row", "col")),
        P(("slab", "row", "col")),
        P(("slab", "row", "col")),
        P(),
        P(),
        P(),
    )
    out_specs = (P(None, "slab", "row", "col"), P())
    return jax.shard_map(shards, mesh=mesh, in_specs=in_specs, out_specs=out_specs, check_vma=False)
```

```python
import jax
import jax.numpy as jnp
from jax import lax
from jax.experimental import pallas as pl
from jax.experimental.pallas import tpu as pltpu
from jax.sharding import PartitionSpec as P

stencil_weights = (
    -5369.0 / 1800.0,
    12.0 / 7.0,
    -15.0 / 56.0,
    10.0 / 189.0,
    -1.0 / 112.0,
    2.0 / 1925.0,
    -1.0 / 16632.0,
)
lower_edge = 3.0
upper_edge = 17.0
centre = 0.5 * (upper_edge + lower_edge)
half_width = 0.5 * (upper_edge - lower_edge)

BANDS = 16
GX, GY, LANES = 32, 64, 128
PX, PY = 6, 8
PITCH = GY + 2 * PY
ROWS = (GX + 2 * PX) * PITCH
TILES = 12
BLOCKS = 32
SLOTS = 8
GROUP = 8
UNROLL = 4
CAP = 2 * BLOCKS * SLOTS
HALO_ROWS = BLOCKS * 34
FAR = -4096
VMEM = pl.BlockSpec(memory_space=pltpu.VMEM)
HIGHEST = lax.Precision.HIGHEST


def lane_of(shape):
    return lax.broadcasted_iota(jnp.int32, shape, len(shape) - 1)


def row_of(shape):
    return lax.broadcasted_iota(jnp.int32, shape, len(shape) - 2)


def pack_kernel(
    positions_in,
    species_in,
    counts_in,
    wave_in,
    potential_in,
    out,
    positions,
    species,
    counts,
    wave,
    potential,
    info,
    sems,
):
    copies = [
        pltpu.make_async_copy(potential_in, potential, sems.at[0]),
        pltpu.make_async_copy(positions_in, positions, sems.at[1]),
        pltpu.make_async_copy(species_in, species, sems.at[2]),
        pltpu.make_async_copy(counts_in, counts, sems.at[3]),
        pltpu.make_async_copy(wave_in.at[0:8], wave.at[0:8], sems.at[4]),
        pltpu.make_async_copy(wave_in.at[8:16], wave.at[8:16], sems.at[5]),
    ]
    for copy in copies:
        copy.start()
    for copy in copies[:4]:
        copy.wait()
    col = lax.axis_index("col")
    low = lane_of((8, LANES)) < 64
    live = lane_of((1, SLOTS)) < counts[...]
    spot = (positions[0:1, :] + PX) * PITCH + positions[1:2, :] + PY
    info[...] = jnp.zeros((8, LANES), jnp.float32)
    info[0:1, 0:SLOTS] = jnp.where(live, positions[2:3, :], FAR).astype(jnp.float32)
    info[1:2, 0:SLOTS] = (spot * 4 + species[...]).astype(jnp.float32)

    def halves(tile, other):
        return (
            jnp.where(low, tile, pltpu.roll(other, 64, 1)),
            jnp.where(low, pltpu.roll(tile, 64, 1), other),
        )

    fixed = [halves(potential[k], potential[k + 4]) for k in range(4)]
    for pair in range(2):
        slabs = [lax.rem(2 * pair + h + col, 4) for h in range(2)]
        copies[4 + pair].wait()

        def one(r, carry):
            band = pair * 8 + r
            for k in range(4):
                parts = halves(wave[band, k], wave[band, k + 4])
                for h in range(2):
                    dest = slabs[h] * 8 + r
                    out[dest, k] = parts[h]
                    out[dest, 4 + k] = fixed[k][h]
            for h in range(2):
                out[slabs[h] * 8 + r, 8] = info[...]
            return carry

        lax.fori_loop(0, 8, one, 0)


def edge_kernel(held, low_out, high_out):
    even = (lane_of((8, LANES)) & 32) == 0

    def one(i, carry):
        for d in [i * UNROLL + k for k in range(UNROLL)]:
            for tile in range(4):
                first = held[d, 2 * tile]
                second = pltpu.roll(held[d, 2 * tile + 1], 32, 1)
                at = pl.multiple_of(d * 32, 32) + tile * 8
                low_out[pl.ds(at, 8), :] = jnp.where(even, first, second)
                high_out[pl.ds(at, 8), :] = jnp.where(even, second, first)
        return carry

    lax.fori_loop(0, BLOCKS // UNROLL, one, 0)
    for k in range(2):
        at = BLOCKS * (32 + k)
        rows = held[:, 8, k, :]
        low_out[at : at + BLOCKS, :] = rows
        high_out[at : at + BLOCKS, :] = rows


def sphere_kernel(offsets, beta, coupling, out):
    points = beta.shape[1]
    for kind in range(beta.shape[0]):
        dx = offsets[3 * kind : 3 * kind + 1, :]
        dy = offsets[3 * kind + 1 : 3 * kind + 2, :]
        dz = offsets[3 * kind + 2 : 3 * kind + 3, :]
        row = 16 + (dx + 3) * 8 + dy + 4
        row = jnp.where(jnp.abs(dx) == 4, jnp.where(dx > 0, 8, 0) + dy + 3, row)
        row = jnp.where(dy == 4, 72 + dx + 3, row)
        row = jnp.where(jnp.abs(dy) == 5, jnp.where(dy > 0, 81, 80), row)
        row = jnp.where(jnp.abs(dx) == 5, jnp.where(dx > 0, 89, 88), row)
        left = (row_of((TILES * 8, points)) == row).astype(jnp.float32)
        values = beta[kind : kind + 1, :] * jnp.sqrt(coupling[0:1, kind : kind + 1])
        right = jnp.where(row_of((LANES, points)) == dz + 5, values, 0.0)
        out[kind] = lax.dot_general(
            left,
            right,
            (((1,), (1,)), ((), ())),
            precision=HIGHEST,
            preferred_element_type=jnp.float32,
        )


def tile_refs(ref, base):
    yield ref.at[pl.ds(base - 4 * PITCH - 3, 8), :]
    yield ref.at[pl.ds(base + 4 * PITCH - 3, 8), :]
    for dx in range(-3, 4):
        yield ref.at[pl.ds(base + dx * PITCH - 4, 8), :]
    yield ref.at[pl.ds(base - 3 * PITCH + 4, 8, stride=PITCH), :]
    yield ref.at[pl.ds(base - 5, 2, stride=10), :]
    yield ref.at[pl.ds(base - 5 * PITCH, 2, stride=10 * PITCH), :]


TILE_ROWS = (8,) * 10 + (2, 2)


def filter_kernel(
    held,
    low_in,
    high_in,
    sphere,
    out,
    buf_a,
    buf_b,
    pot,
    rolled,
    acc,
    total,
    table_v,
    table,
    listed,
    sem,
):
    slab, col = lax.axis_index("slab"), lax.axis_index("col")
    half = lax.rem(slab + 4 - lax.rem(col, 4), 4) % 2
    depth = col * 2 + half
    lane8, row8 = lane_of((8, LANES)), row_of((8, LANES))

    both = []
    for k in range(2):
        at = BLOCKS * (32 + k)
        outer = jnp.where(half == 0, low_in[at : at + BLOCKS, :], high_in[at : at + BLOCKS, :])
        both.append(jnp.concatenate([held[:, 8, k, :], outer], axis=0).astype(jnp.int32))
    along, spot = both
    along = along - (depth * 64 - 32)
    code = jnp.where((along >= 7) & (along < 121), 2, 3)
    code = code - jnp.where((along >= 17) & (along < 111), 1, 0)
    code = code - jnp.where((along >= 27) & (along < 101), 1, 0)
    code = jnp.where(spot > 0, code, 3)
    turn = (along - 37) & (LANES - 1)
    table_v[...] = jnp.where(code < 3, spot * 512 + turn * 4 + code, 3)
    copy = pltpu.make_async_copy(table_v, table, sem)
    copy.start()

    edge = PX * PITCH

    def clear_edges(target):
        target[0:edge, :] = jnp.zeros((edge, LANES), jnp.float32)
        target[ROWS - edge :, :] = jnp.zeros((edge, LANES), jnp.float32)

        for x in range(PX, PX + GX):
            at = x * PITCH
            target[at : at + PY, :] = jnp.zeros((PY, LANES), jnp.float32)
            target[at + PY + GY : at + PITCH, :] = jnp.zeros((PY, LANES), jnp.float32)

    clear_edges(buf_a)
    copy.wait()

    low = lane8 < 64
    even = (lane8 & 32) == 0

    def gather_block(d):
        s, r = d // 8, lax.rem(d, 8)
        for field in range(2):
            for pair in range(2):
                at = pl.multiple_of(d * 32, 32) + field * 16 + pair * 8
                above = high_in[pl.ds(at, 8), :]
                below = low_in[pl.ds(at, 8), :]
                evens = jnp.where(even, above, below)
                odds = jnp.where(even, below, above)
                turned = (
                    pltpu.roll(evens, 64, 1),
                    pltpu.roll(odds, 32, 1),
                    evens,
                    pltpu.roll(odds, 96, 1),
                )
                for m in range(2):
                    own = held[d, field * 4 + 2 * pair + m]
                    for high in range(2):
                        x = 4 * high + 2 * pair + m
                        mid = pltpu.roll(own, 64, 1) if high else own
                        tile = jnp.where(low, mid, turned[2 * high + m])
                        if field == 0:
                            to = pl.multiple_of((s * 8 + x + PX) * PITCH + PY + r * 8, 8)
                            buf_a[pl.ds(to, 8), :] = tile
                        else:
                            to = pl.multiple_of((s * 8 + x) * GY + r * 8, 8)
                            pot[pl.ds(to, 8), :] = tile - (centre + stencil_weights[0])

    def blocks(i, lengths):
        for k in range(UNROLL):
            gather_block(i * UNROLL + k)
        words = [
            table[2 * UNROLL * i + k, slot] for k in range(2 * UNROLL) for slot in range(SLOTS)
        ]
        for word in words:
            code = word & 3
            shift = code * 10
            listed[(lax.shift_right_logical(lengths, shift) & 1023) + code * CAP] = word
            lengths = lengths + lax.shift_left(jnp.int32(1), shift)
        return lengths

    lengths = lax.fori_loop(0, BLOCKS // UNROLL, blocks, jnp.int32(0))
    n3, n2, n1 = lengths & 1023, (lengths >> 10) & 1023, (lengths >> 20) & 1023

    def move_second(i, carry):
        listed[n3 + i] = listed[CAP + i]
        return carry

    def move_first(i, carry):
        listed[n3 + n2 + i] = listed[2 * CAP + i]
        return carry

    lax.fori_loop(0, n2, move_second, 0)
    lax.fori_loop(0, n1, move_first, 0)
    for i in range(GROUP - 1):
        listed[n3 + n2 + n1 + i] = (edge + PY) << 11

    apart = jnp.abs(lane_of((LANES, LANES)) - row_of((LANES, LANES)))
    apart = jnp.minimum(apart, LANES - apart)
    band = jnp.zeros((LANES, LANES), jnp.float32)
    for reach in range(7):
        band = jnp.where(apart == reach, -0.5 * stencil_weights[reach], band)
    band_high = band.astype(jnp.bfloat16)
    band_low = (band - band_high.astype(jnp.float32)).astype(jnp.bfloat16)
    band = jnp.concatenate(
        [
            jnp.concatenate([band_high, band_low], axis=1),
            jnp.concatenate([band_high, jnp.zeros_like(band_low)], axis=1),
        ],
        axis=0,
    )

    lanes = lane_of((1, LANES))
    outside = ((lanes >= 96) & (depth == 0)) | ((lanes >= 64) & (lanes < 96) & (depth == 15))
    mask = jnp.where(outside, 0.0, 1.0)

    def local_part(source, target, scale, subtract):
        factor = mask * scale

        def one(r, carry):
            row = pl.multiple_of(r * 8, 8) + PY
            line = [source[pl.ds(row + x * PITCH, 8), :] for x in range(GX + 2 * PX)]
            field = jnp.concatenate(line[PX : PX + GX], axis=0)
            high = field.astype(jnp.bfloat16)
            small = (field - high.astype(jnp.float32)).astype(jnp.bfloat16)
            both = jnp.concatenate([high, small], axis=1)
            part = jnp.dot(both, band, preferred_element_type=jnp.float32)
            part = part[:, :LANES] + part[:, LANES:]
            for x in range(GX):
                at = row + (x + PX) * PITCH
                own = line[x + PX]
                result = part[8 * x : 8 * x + 8] + pot[pl.ds(row - PY + x * GY, 8), :] * own
                for reach in range(1, 7):
                    near = line[x + PX - reach] + line[x + PX + reach]
                    near += source[pl.ds(at - reach, 8), :] + source[pl.ds(at + reach, 8), :]
                    result += (-0.5 * stencil_weights[reach]) * near
                result = result * factor
                if subtract:
                    result -= target[pl.ds(at, 8), :]
                target[pl.ds(at, 8), :] = result
            return carry

        lax.fori_loop(0, GY // 8, one, 0)

    def gather_atoms(source, count, first):
        def one(i, carry):
            sums = []
            for j in [i * GROUP + k for k in range(GROUP)]:
                word = listed[j]
                base = word >> 11
                kind = (word >> 9) & 3
                turn = (word >> 2) & 127
                parts = []
                for t, ref in enumerate(tile_refs(source, base)):
                    rows = slice(8 * t, 8 * t + TILE_ROWS[t])
                    if first:
                        shape = pltpu.roll(sphere[kind, rows, :], turn, 1) * mask
                        rolled[j, rows, :] = shape
                    else:
                        shape = rolled[j, rows, :]
                    parts.append(ref[...] * shape)
                small = parts[10] + parts[11]
                parts[10:] = [jnp.concatenate([small, jnp.zeros((6, LANES), jnp.float32)], axis=0)]
                while len(parts) > 1:
                    rest = parts[len(parts) // 2 * 2 :]
                    parts = [a + b for a, b in zip(parts[::2], parts[1::2])] + rest
                sums.append(parts[0])
            for width in (1, 2, 4):
                keep = (row8 & width) == 0
                sums = [
                    jnp.where(keep, a, b) + pltpu.roll(jnp.where(keep, b, a), width, 0)
                    for a, b in zip(sums[::2], sums[1::2])
                ]
            acc[i] = sums[0]
            return carry

        lax.fori_loop(0, (count + GROUP - 1) // GROUP, one, 0)

    def sum_atoms(count, scale):
        size = 8 * GROUP

        def one(i, carry):
            at = pl.multiple_of(i * size, size)
            part = acc[pl.ds(pl.multiple_of(i * 8, 8), 8)].reshape(size, LANES)
            part = jnp.sum(part, axis=1, keepdims=True) * scale
            total[pl.ds(at, size), :] = jnp.broadcast_to(part, (size, LANES))
            return carry

        lax.fori_loop(0, (count + size - 1) // size, one, 0)

    def spread_atoms(target, count):
        def one(j, carry):
            base = listed[j] >> 11
            q = total[pl.ds(j, 1), :]
            refs = list(tile_refs(target, base))
            values = []
            for t, ref in enumerate(refs):
                size = TILE_ROWS[t]
                values.append(ref[...] + q * rolled[j, 8 * t : 8 * t + size, :])
            for ref, value in zip(refs, values):
                ref[...] = value
            return carry

        lax.fori_loop(0, count, one, 0)

    def step(source, target, scale, subtract, count, first):
        gather_atoms(source, count, first)
        sum_atoms(count, scale)
        local_part(source, target, scale, subtract)
        spread_atoms(target, count)

    step(buf_a, buf_b, 1.0 / half_width, False, n3 + n2 + n1, True)
    clear_edges(buf_b)
    step(buf_b, buf_a, 2.0 / half_width, True, n3 + n2, False)
    clear_edges(buf_a)
    step(buf_a, buf_b, 2.0 / half_width, True, n3, False)

    def send_blocks(i, carry):
        for d in [i * UNROLL + k for k in range(UNROLL)]:
            s, r = d // 8, lax.rem(d, 8)
            for k in range(4):
                at = pl.multiple_of((s * 8 + k + PX) * PITCH + PY + r * 8, 8)
                first = buf_b[pl.ds(at, 8), :]
                second = buf_b[pl.ds(at + 4 * PITCH, 8), :]
                out[d, k] = jnp.where(low, first, pltpu.roll(second, 64, 1))
        return carry

    lax.fori_loop(0, BLOCKS // UNROLL, send_blocks, 0)


def dot(a, b, dims):
    return lax.dot_general(
        a, b, (dims, ((), ())), precision=HIGHEST, preferred_element_type=jnp.float32
    )


def unpack_kernel(held, out, gram):
    col = lax.axis_index("col")
    low = lane_of((8, LANES)) < 64
    for pair in range(2):
        slabs = [lax.rem(2 * pair + h + col, 4) for h in range(2)]

        def one(i, carry):
            for r in [i * UNROLL + k for k in range(UNROLL)]:
                for k in range(4):
                    first = held[slabs[0] * 8 + r, k]
                    second = held[slabs[1] * 8 + r, k]
                    out[pair * 8 + r, k] = jnp.where(low, first, pltpu.roll(second, 64, 1))
                    out[pair * 8 + r, k + 4] = jnp.where(low, pltpu.roll(first, 64, 1), second)
            return carry

        lax.fori_loop(0, 8 // UNROLL, one, 0)

    size = BANDS * 8
    products = jnp.zeros((size, size), jnp.float32)
    for x in range(8):
        plane = out[:, x].reshape(size, LANES)
        products += dot(plane, plane, ((1,), (1,)))
    row, lane = row_of((size, size)), lane_of((size, size))
    products = jnp.where((row & 7) == (lane & 7), products, 0.0)
    pick = (row_of((BANDS, size)) == lane_of((BANDS, size)) // 8).astype(jnp.float32)
    rows = dot(pick, products, ((1,), (0,)))
    spread = (row_of((size, LANES)) // 8 == (lane_of((size, LANES)) & 15)).astype(jnp.float32)
    square = dot(rows, spread, ((1,), (0,)))
    own = (row_of((BANDS, LANES)) & 7) == lane_of((BANDS, LANES)) // BANDS
    square = jnp.where(own, square, 0.0)
    both = [jnp.sum(square[8 * k : 8 * k + 8], axis=0, keepdims=True) for k in range(2)]
    gram[...] = jnp.concatenate(both * (gram.shape[0] // 2), axis=0)


def sum_copies(parts):
    tiles = [parts[8 * i : 8 * i + 8, :] for i in range(parts.shape[0] // 8)]
    while len(tiles) > 1:
        tiles = [a + b for a, b in zip(tiles[::2], tiles[1::2])]
    total = tiles[0] + pltpu.roll(tiles[0], 4, 0)
    return total + pltpu.roll(total, 2, 0)


def middle_kernel(parts, out):
    total = sum_copies(parts)
    for i in range(out.shape[0] // 8):
        out[8 * i : 8 * i + 8, :] = total


def total_kernel(parts, out):
    total = sum_copies(parts)
    rows = jnp.where(row_of((BANDS, LANES)) < 8, total[0:1], total[1:2])
    own = (row_of((BANDS, LANES)) & 7) == lane_of((BANDS, LANES)) // BANDS
    fold = (row_of((LANES, BANDS)) & 15) == lane_of((LANES, BANDS))
    square = dot(jnp.where(own, rows, 0.0), fold.astype(jnp.float32), ((1,), (0,)))
    out[...] = square * (1.0 / (GX * GY * 1024))


def in_hbm(x):
    return pltpu.with_memory_space_constraint(x, pltpu.HBM)


def f32(*shape):
    return jax.ShapeDtypeStruct(shape, jnp.float32)


def params(mib=None):
    return pltpu.CompilerParams(vmem_limit_bytes=None if mib is None else mib << 20)


def filter_call(held, low_in, high_in, sphere):
    return pl.pallas_call(
        filter_kernel,
        out_shape=f32(BLOCKS, 4, 8, LANES),
        in_specs=[VMEM] * 4,
        out_specs=VMEM,
        scratch_shapes=[
            pltpu.VMEM((ROWS, LANES), jnp.float32),
            pltpu.VMEM((ROWS, LANES), jnp.float32),
            pltpu.VMEM((GX * GY, LANES), jnp.float32),
            pltpu.VMEM((CAP + GROUP, TILES * 8, LANES), jnp.float32),
            pltpu.VMEM((CAP // GROUP, 8, LANES), jnp.float32),
            pltpu.VMEM((CAP, LANES), jnp.float32),
            pltpu.VMEM((2 * BLOCKS, LANES), jnp.int32),
            pltpu.SMEM((2 * BLOCKS, LANES), jnp.int32),
            pltpu.SMEM((3 * CAP + 1024,), jnp.int32),
            pltpu.SemaphoreType.DMA,
        ],
        compiler_params=params(40),
        name="filter",
    )(held, low_in, high_in, sphere)


def shards(wave, potential, positions, species, counts, offsets, beta, coupling):
    packed = pl.pallas_call(
        pack_kernel,
        out_shape=f32(BLOCKS, 9, 8, LANES),
        in_specs=[pl.BlockSpec(memory_space=pltpu.HBM)] * 5,
        out_specs=VMEM,
        scratch_shapes=[
            pltpu.VMEM(positions.shape, jnp.int32),
            pltpu.VMEM((1, SLOTS), jnp.int32),
            pltpu.VMEM((1, 1), jnp.int32),
            pltpu.VMEM(wave.shape, jnp.float32),
            pltpu.VMEM(potential.shape, jnp.float32),
            pltpu.VMEM((8, LANES), jnp.float32),
            pltpu.SemaphoreType.DMA((6,)),
        ],
        compiler_params=params(16),
        name="pack",
    )(in_hbm(positions), in_hbm(species[None]), counts[None], in_hbm(wave), in_hbm(potential))
    held = lax.all_to_all(packed, ("slab", "row"), split_axis=0, concat_axis=0, tiled=True)

    low_edge, high_edge = pl.pallas_call(
        edge_kernel,
        out_shape=(f32(HALO_ROWS, LANES), f32(HALO_ROWS, LANES)),
        in_specs=[VMEM],
        out_specs=(VMEM, VMEM),
        compiler_params=params(16),
        name="edges",
    )(held)

    order = [((h + 2 * pair + col) % 4) * 8 + col for pair in range(2) for col in range(8) for h in range(2)]
    chains = (order[:16], order[16:])
    up = [(a, b) for chain in chains for a, b in zip(chain[:-1], chain[1:])]
    down = [(b, a) for a, b in up]
    low_in = lax.ppermute(high_edge, ("slab", "col"), up)
    high_in = lax.ppermute(low_edge, ("slab", "col"), down)

    sphere = pl.pallas_call(
        sphere_kernel,
        out_shape=pltpu.VMEM((beta.shape[0], TILES * 8, LANES), jnp.float32),
        in_specs=[VMEM, VMEM, VMEM],
        out_specs=VMEM,
        name="sphere",
    )(offsets.reshape(-1, offsets.shape[2]), beta, coupling[None])

    filtered = filter_call(held, low_in, high_in, sphere)
    back = lax.all_to_all(filtered, ("slab", "row"), split_axis=0, concat_axis=0, tiled=True)
    result, partial = pl.pallas_call(
        unpack_kernel,
        out_shape=(f32(*wave.shape), f32(512, LANES)),
        in_specs=[VMEM],
        out_specs=(VMEM, VMEM),
        compiler_params=params(16),
        name="unpack",
    )(back)

    parts = lax.all_to_all(
        partial, ("slab", "row", "col"), split_axis=0, concat_axis=0, tiled=True
    )
    gram = pl.pallas_call(
        total_kernel,
        out_shape=f32(BANDS, BANDS),
        in_specs=[VMEM],
        out_specs=VMEM,
        name="total",
    )(parts)
    return result, gram


def solution(mesh):
    in_specs = (
        P(None, "slab", "row", "col"),
        P("slab", "row", "col"),
        P(None, ("slab", "row", "col")),
        P(("slab", "row", "col")),
        P(("slab", "row", "col")),
        P(),
        P(),
        P(),
    )
    out_specs = (P(None, "slab", "row", "col"), P())
    return jax.shard_map(shards, mesh=mesh, in_specs=in_specs, out_specs=out_specs, check_vma=False)
```

```python
import jax
import jax.numpy as jnp
from jax import lax
from jax.experimental import pallas as pl
from jax.experimental.pallas import tpu as pltpu
from jax.sharding import PartitionSpec as P

stencil_weights = (
    -5369.0 / 1800.0,
    12.0 / 7.0,
    -15.0 / 56.0,
    10.0 / 189.0,
    -1.0 / 112.0,
    2.0 / 1925.0,
    -1.0 / 16632.0,
)
lower_edge = 3.0
upper_edge = 17.0
centre = 0.5 * (upper_edge + lower_edge)
half_width = 0.5 * (upper_edge - lower_edge)

BANDS = 16
GX, GY, LANES = 32, 64, 128
PX, PY = 6, 8
PITCH = GY + 2 * PY
ROWS = (GX + 2 * PX) * PITCH
TILES = 11
BLOCKS = 32
SLOTS = 8
GROUP = 8
UNROLL = 4
CAP = BLOCKS * SLOTS
LIST = 1024
HALO_ROWS = BLOCKS * 33
VMEM = pl.BlockSpec(memory_space=pltpu.VMEM)
HIGHEST = lax.Precision.HIGHEST


def lane_of(shape):
    return lax.broadcasted_iota(jnp.int32, shape, len(shape) - 1)


def row_of(shape):
    return lax.broadcasted_iota(jnp.int32, shape, len(shape) - 2)


def pack_kernel(
    positions_in,
    species_in,
    counts_in,
    wave_in,
    potential_in,
    out,
    positions,
    species,
    counts,
    wave,
    potential,
    info,
    sems,
):
    copies = [
        pltpu.make_async_copy(potential_in, potential, sems.at[0]),
        pltpu.make_async_copy(positions_in, positions, sems.at[1]),
        pltpu.make_async_copy(species_in, species, sems.at[2]),
        pltpu.make_async_copy(counts_in, counts, sems.at[3]),
    ]
    for piece in range(4):
        bands = pl.ds(4 * piece, 4)
        copies.append(
            pltpu.make_async_copy(wave_in.at[bands], wave.at[bands], sems.at[4 + piece])
        )
    for copy in copies:
        copy.start()
    for copy in copies[:4]:
        copy.wait()
    col = lax.axis_index("col")
    low = lane_of((8, LANES)) < 64
    live = jnp.where(lane_of((1, SLOTS)) < counts[...], 1, 0)
    rows = [positions[k : k + 1, :] for k in range(3)] + [species[...], live]
    info[...] = jnp.zeros((8, LANES), jnp.float32)
    for k, values in enumerate(rows):
        info[0:1, SLOTS * k : SLOTS * (k + 1)] = values.astype(jnp.float32)

    def halves(tile, other):
        return (
            jnp.where(low, tile, pltpu.roll(other, 64, 1)),
            jnp.where(low, pltpu.roll(tile, 64, 1), other),
        )

    fixed = [halves(potential[k], potential[k + 4]) for k in range(4)]
    for pair in range(2):
        slabs = [lax.rem(2 * pair + h + col, 4) for h in range(2)]
        for r in range(8):
            if r % 4 == 0:
                copies[4 + 2 * pair + r // 4].wait()
            band = pair * 8 + r
            for k in range(4):
                parts = halves(wave[band, k], wave[band, k + 4])
                for h in range(2):
                    dest = slabs[h] * 8 + r
                    out[dest, k] = parts[h]
                    out[dest, 4 + k] = fixed[k][h]
            for h in range(2):
                out[slabs[h] * 8 + r, 8] = info[...]


def edge_kernel(held, low_out, high_out):
    even = (lane_of((8, LANES)) & 32) == 0

    def one(i, carry):
        for d in [i * UNROLL + k for k in range(UNROLL)]:
            for tile in range(4):
                first = held[d, 2 * tile]
                second = pltpu.roll(held[d, 2 * tile + 1], 32, 1)
                at = pl.multiple_of(d * 32, 32) + tile * 8
                low_out[pl.ds(at, 8), :] = jnp.where(even, first, second)
                high_out[pl.ds(at, 8), :] = jnp.where(even, second, first)
        return carry

    lax.fori_loop(0, BLOCKS // UNROLL, one, 0)
    rows = held[:, 8, 0, :]
    low_out[BLOCKS * 32 :, :] = rows
    high_out[BLOCKS * 32 :, :] = rows


def fill_sphere(offsets, beta, coupling, out):
    points = beta.shape[1]
    for kind in range(beta.shape[0]):
        dx = offsets[3 * kind : 3 * kind + 1, :]
        dy = offsets[3 * kind + 1 : 3 * kind + 2, :]
        dz = offsets[3 * kind + 2 : 3 * kind + 3, :]
        row = 16 + (dx + 3) * 8 + dy + 4
        row = jnp.where(jnp.abs(dx) == 4, jnp.where(dx > 0, 8, 0) + dy + 3, row)
        row = jnp.where(dy == 4, 72 + dx + 3, row)
        row = jnp.where(jnp.abs(dy) == 5, jnp.where(dy > 0, 81, 80), row)
        row = jnp.where(jnp.abs(dx) == 5, jnp.where(dx > 0, 83, 82), row)
        left = (row_of((TILES * 8, points)) == row).astype(jnp.float32)
        values = beta[kind : kind + 1, :] * jnp.sqrt(coupling[0:1, kind : kind + 1])
        right = jnp.where(row_of((LANES, points)) == dz + 5, values, 0.0)
        out[kind] = lax.dot_general(
            left,
            right,
            (((1,), (1,)), ((), ())),
            precision=HIGHEST,
            preferred_element_type=jnp.float32,
        )


def tile_refs(ref, base):
    yield ref.at[pl.ds(base - 4 * PITCH - 3, 8), :]
    yield ref.at[pl.ds(base + 4 * PITCH - 3, 8), :]
    for dx in range(-3, 4):
        yield ref.at[pl.ds(base + dx * PITCH - 4, 8), :]
    yield ref.at[pl.ds(base - 3 * PITCH + 4, 8, stride=PITCH), :]
    yield ref.at[pl.ds(base - 5, 2, stride=10), :]
    yield ref.at[pl.ds(base - 5 * PITCH, 2, stride=10 * PITCH), :]


TILE_ROWS = (8,) * 10 + (2, 2)
TILE_AT = tuple(8 * t for t in range(11)) + (82,)


def place_along_z():
    slab, col = lax.axis_index("slab"), lax.axis_index("col")
    half = lax.rem(slab + 4 - lax.rem(col, 4), 4) % 2
    return half, col * 2 + half


def atom_words(rows, depth):
    rows = rows.astype(jnp.int32)
    x, y, along, kind, live = (
        rows if k == 0 else pltpu.roll(rows, LANES - SLOTS * k, 1) for k in range(5)
    )
    along = along - (depth * 64 - 32)
    code = jnp.where((along >= 7) & (along < 121), 2, 3)
    code = code - jnp.where((along >= 17) & (along < 111), 1, 0)
    code = code - jnp.where((along >= 27) & (along < 101), 1, 0)
    code = jnp.where(live > 0, code, 3)
    turn = (along - 37) & (LANES - 1)
    spot = (x + PX) * PITCH + y + PY
    return jnp.where(code < 3, (spot * 4 + kind) * 512 + turn * 4 + code, 3)


def list_rows(table, listed, first_row, count, lengths):
    words = [table[first_row + k, slot] for k in range(count) for slot in range(SLOTS)]
    for word in words:
        code = word & 3
        shift = code * 10
        listed[(lax.shift_right_logical(lengths, shift) & 1023) + code * CAP] = word
        lengths = lengths + lax.shift_left(jnp.int32(1), shift)
    return lengths


def join_lists(listed, lengths):
    n0, n1, n2 = lengths & 1023, (lengths >> 10) & 1023, (lengths >> 20) & 1023

    def move_second(i, carry):
        listed[n0 + i] = listed[CAP + i]
        return carry

    def move_third(i, carry):
        listed[n0 + n1 + i] = listed[2 * CAP + i]
        return carry

    lax.fori_loop(0, n1, move_second, 0)
    lax.fori_loop(0, n2, move_third, 0)
    for i in range(GROUP - 1):
        listed[n0 + n1 + n2 + i] = (PX * PITCH + PY) << 11
    return n0 + n1 + n2, n0 + n1, n0


def lane_mask(depth):
    lanes = lane_of((1, LANES))
    outside = ((lanes >= 96) & (depth == 0)) | ((lanes >= 64) & (lanes < 96) & (depth == 15))
    return jnp.where(outside, 0.0, 1.0)


def turn_sphere(sphere, word, mask, rolled, j):
    kind = (word >> 9) & 3
    turn = (word >> 2) & 127
    for t in range(TILES):
        rows = slice(8 * t, 8 * t + 8)
        rolled[j, rows, :] = pltpu.roll(sphere[kind, rows, :], turn, 1) * mask


def atoms_kernel(
    held, offsets, beta, coupling, sphere, rolled, list_out, table_v, table, listed, sems
):
    half, depth = place_along_z()
    table_v[...] = atom_words(held[:, 8, 0, :], depth)
    copy = pltpu.make_async_copy(table_v, table, sems.at[0])
    copy.start()
    fill_sphere(offsets, beta, coupling, sphere)
    copy.wait()

    def build(i, lengths):
        return list_rows(table, listed, 4 * i, 4, lengths)

    lengths = lax.fori_loop(0, BLOCKS // 4, build, jnp.int32(0))
    counts = join_lists(listed, lengths)
    for k in range(3):
        listed[LIST - 3 + k] = counts[k]
    copy = pltpu.make_async_copy(listed.at[pl.ds(0, LIST)], list_out, sems.at[1])
    copy.start()
    mask = lane_mask(depth)

    def turn_group(i, carry):
        for j in [i * 4 + k for k in range(4)]:
            turn_sphere(sphere, listed[j], mask, rolled, j)
        return carry

    lax.fori_loop(0, (counts[0] + 3) // 4, turn_group, 0)
    copy.wait()


def filter_kernel(
    held,
    low_in,
    high_in,
    sphere,
    rolled,
    list_in,
    out,
    buf_a,
    buf_b,
    pot,
    parts,
    outer_rolled,
    acc,
    total,
    table_v,
    table,
    listed,
    outer_listed,
    sems,
):
    half, depth = place_along_z()
    lane8, row8 = lane_of((8, LANES)), row_of((8, LANES))

    outer = jnp.where(half == 0, low_in[BLOCKS * 32 :, :], high_in[BLOCKS * 32 :, :])
    table_v[...] = atom_words(outer, depth)
    copies = [
        pltpu.make_async_copy(table_v, table, sems.at[0]),
        pltpu.make_async_copy(list_in, listed, sems.at[1]),
    ]
    for copy in copies:
        copy.start()

    edge = PX * PITCH

    def clear_edges(target):
        target[0:edge, :] = jnp.zeros((edge, LANES), jnp.float32)
        target[ROWS - edge :, :] = jnp.zeros((edge, LANES), jnp.float32)

        for x in range(PX, PX + GX):
            at = x * PITCH
            target[at : at + PY, :] = jnp.zeros((PY, LANES), jnp.float32)
            target[at + PY + GY : at + PITCH, :] = jnp.zeros((PY, LANES), jnp.float32)

    clear_edges(buf_a)
    for copy in copies:
        copy.wait()

    low = lane8 < 64
    even = (lane8 & 32) == 0

    def gather_block(d):
        s, r = d // 8, lax.rem(d, 8)
        for field in range(2):
            for pair in range(2):
                at = pl.multiple_of(d * 32, 32) + field * 16 + pair * 8
                above = high_in[pl.ds(at, 8), :]
                below = low_in[pl.ds(at, 8), :]
                evens = jnp.where(even, above, below)
                odds = jnp.where(even, below, above)
                turned = (
                    pltpu.roll(evens, 64, 1),
                    pltpu.roll(odds, 32, 1),
                    evens,
                    pltpu.roll(odds, 96, 1),
                )
                for m in range(2):
                    own = held[d, field * 4 + 2 * pair + m]
                    for high in range(2):
                        x = 4 * high + 2 * pair + m
                        mid = pltpu.roll(own, 64, 1) if high else own
                        tile = jnp.where(low, mid, turned[2 * high + m])
                        if field == 0:
                            to = pl.multiple_of((s * 8 + x + PX) * PITCH + PY + r * 8, 8)
                            buf_a[pl.ds(to, 8), :] = tile
                        else:
                            to = pl.multiple_of((s * 8 + x) * GY + r * 8, 8)
                            pot[pl.ds(to, 8), :] = tile - (centre + 1.5 * stencil_weights[0])

    def blocks(i, lengths):
        for k in range(UNROLL):
            gather_block(i * UNROLL + k)
        return list_rows(table, outer_listed, UNROLL * i, UNROLL, lengths)

    lengths = lax.fori_loop(0, BLOCKS // UNROLL, blocks, jnp.int32(0))
    outer_counts = join_lists(outer_listed, lengths)
    own_counts = [listed[LIST - 3 + k] for k in range(3)]
    own_groups = (own_counts[0] + GROUP - 1) // GROUP

    apart = jnp.abs(lane_of((LANES, LANES)) - row_of((LANES, LANES)))
    apart = jnp.minimum(apart, LANES - apart)
    band = jnp.zeros((LANES, LANES), jnp.float32)
    for reach in range(1, 7):
        band = jnp.where(apart == reach, -0.5 * stencil_weights[reach], band)
    z_high = band.astype(jnp.bfloat16)
    z_low = (band - z_high.astype(jnp.float32)).astype(jnp.bfloat16)
    z_band = jnp.concatenate(
        [
            jnp.concatenate([z_high, z_low], axis=1),
            jnp.concatenate([z_high, jnp.zeros_like(z_low)], axis=1),
        ],
        axis=0,
    )
    planes = 4
    mask = lane_mask(depth)

    def products(source, g, slot):
        first = g * (planes * PITCH) + PX * PITCH + PY
        field = jnp.concatenate(
            [source[pl.ds(first + x * PITCH, GY), :] for x in range(planes)], axis=0
        )
        high = field.astype(jnp.bfloat16)
        small = (field - high.astype(jnp.float32)).astype(jnp.bfloat16)
        both = jnp.concatenate([high, small], axis=1)
        along_z = jnp.dot(both, z_band, preferred_element_type=jnp.float32)
        parts[slot] = along_z[:, :LANES] + along_z[:, LANES:]

    def local_part(source, target, scale, subtract):
        factor = mask * scale

        def one(g, carry, more=True):
            slot = g & 1
            first = g * (planes * PITCH) + PX * PITCH + PY
            for t in range(GY // 8):
                line = [
                    source[pl.ds(first + (x - PX) * PITCH + 8 * t, 8), :]
                    for x in range(planes + 2 * PX)
                ]
                for x in range(planes):
                    at = x * GY + 8 * t
                    own_at = g * (planes * GY) + at
                    to = first + x * PITCH + 8 * t
                    result = parts[slot, at : at + 8, :] + pot[pl.ds(own_at, 8), :] * line[x + PX]
                    for reach in range(1, 7):
                        near = line[x + PX - reach] + line[x + PX + reach]
                        near += source[pl.ds(to - reach, 8), :] + source[pl.ds(to + reach, 8), :]
                        result += (-0.5 * stencil_weights[reach]) * near
                    result = result * factor
                    if subtract:
                        result -= target[pl.ds(to, 8), :]
                    target[pl.ds(to, 8), :] = result
            if more:
                products(source, g + 1, 1 - slot)
            return carry

        products(source, 0, 0)
        for g in range(GX // planes):
            one(g, 0, g < GX // planes - 1)

    def gather_atoms(source, atoms, tables, count, first_group, turn):
        def one(i, carry):
            sums = []
            for j in [i * GROUP + k for k in range(GROUP)]:
                word = atoms[j]
                if turn:
                    turn_sphere(sphere, word, mask, tables, j)
                terms = []
                for t, ref in enumerate(tile_refs(source, word >> 11)):
                    terms.append(ref[...] * tables[j, TILE_AT[t] : TILE_AT[t] + TILE_ROWS[t], :])
                small = terms[10] + terms[11]
                terms[10:] = [jnp.concatenate([small, jnp.zeros((6, LANES), jnp.float32)], axis=0)]
                while len(terms) > 1:
                    rest = terms[len(terms) // 2 * 2 :]
                    terms = [a + b for a, b in zip(terms[::2], terms[1::2])] + rest
                sums.append(terms[0])
            for width in (1, 2, 4):
                keep = (row8 & width) == 0
                sums = [
                    jnp.where(keep, a, b) + pltpu.roll(jnp.where(keep, b, a), width, 0)
                    for a, b in zip(sums[::2], sums[1::2])
                ]
            acc[first_group + i] = sums[0]
            return carry

        lax.fori_loop(0, (count + GROUP - 1) // GROUP, one, 0)

    def sum_atoms(count, scale):
        size = 8 * GROUP

        def one(i, carry):
            at = pl.multiple_of(i * size, size)
            part = acc[pl.ds(pl.multiple_of(i * 8, 8), 8)].reshape(size, LANES)
            part = jnp.sum(part, axis=1, keepdims=True) * scale
            total[pl.ds(at, size), :] = jnp.broadcast_to(part, (size, LANES))
            return carry

        lax.fori_loop(0, (count + size - 1) // size, one, 0)

    def spread_atoms(target, atoms, tables, count, first):
        def one(j, carry):
            q = total[pl.ds(first + j, 1), :]
            refs = list(tile_refs(target, atoms[j] >> 11))
            values = []
            for t, ref in enumerate(refs):
                values.append(ref[...] + q * tables[j, TILE_AT[t] : TILE_AT[t] + TILE_ROWS[t], :])
            for ref, value in zip(refs, values):
                ref[...] = value
            return carry

        lax.fori_loop(0, count, one, 0)

    def step(source, target, scale, subtract, which):
        own, outer = own_counts[which], outer_counts[which]
        gather_atoms(source, listed, rolled, own, 0, False)
        gather_atoms(source, outer_listed, outer_rolled, outer, own_groups, which == 0)
        sum_atoms(own_groups * GROUP + outer, scale)
        local_part(source, target, scale, subtract)
        spread_atoms(target, listed, rolled, own, 0)
        spread_atoms(target, outer_listed, outer_rolled, outer, own_groups * GROUP)

    step(buf_a, buf_b, 1.0 / half_width, False, 0)
    clear_edges(buf_b)
    step(buf_b, buf_a, 2.0 / half_width, True, 1)
    clear_edges(buf_a)
    step(buf_a, buf_b, 2.0 / half_width, True, 2)

    def send_blocks(i, carry):
        for d in [i * UNROLL + k for k in range(UNROLL)]:
            s, r = d // 8, lax.rem(d, 8)
            for k in range(4):
                at = pl.multiple_of((s * 8 + k + PX) * PITCH + PY + r * 8, 8)
                first = buf_b[pl.ds(at, 8), :]
                second = buf_b[pl.ds(at + 4 * PITCH, 8), :]
                out[d, k] = jnp.where(low, first, pltpu.roll(second, 64, 1))
        return carry

    lax.fori_loop(0, BLOCKS // UNROLL, send_blocks, 0)


def dot(a, b, dims):
    return lax.dot_general(
        a, b, (dims, ((), ())), precision=HIGHEST, preferred_element_type=jnp.float32
    )


def unpack_kernel(held, out, gram):
    col = lax.axis_index("col")
    low = lane_of((8, LANES)) < 64
    for pair in range(2):
        slabs = [lax.rem(2 * pair + h + col, 4) for h in range(2)]

        def one(i, carry):
            for r in [i * UNROLL + k for k in range(UNROLL)]:
                for k in range(4):
                    first = held[slabs[0] * 8 + r, k]
                    second = held[slabs[1] * 8 + r, k]
                    out[pair * 8 + r, k] = jnp.where(low, first, pltpu.roll(second, 64, 1))
                    out[pair * 8 + r, k + 4] = jnp.where(low, pltpu.roll(first, 64, 1), second)
            return carry

        lax.fori_loop(0, 8 // UNROLL, one, 0)

    size = BANDS * 8
    products = jnp.zeros((size, size), jnp.float32)
    for x in range(8):
        plane = out[:, x].reshape(size, LANES)
        products += dot(plane, plane, ((1,), (1,)))
    row, lane = row_of((size, size)), lane_of((size, size))
    products = jnp.where((row & 7) == (lane & 7), products, 0.0)
    pick = (row_of((BANDS, size)) == lane_of((BANDS, size)) // 8).astype(jnp.float32)
    rows = dot(pick, products, ((1,), (0,)))
    spread = (row_of((size, LANES)) // 8 == (lane_of((size, LANES)) & 15)).astype(jnp.float32)
    square = dot(rows, spread, ((1,), (0,)))
    own = (row_of((BANDS, LANES)) & 7) == lane_of((BANDS, LANES)) // BANDS
    square = jnp.where(own, square, 0.0)
    both = [jnp.sum(square[8 * k : 8 * k + 8], axis=0, keepdims=True) for k in range(2)]
    gram[...] = jnp.concatenate(both * (gram.shape[0] // 2), axis=0)


def sum_copies(parts):
    tiles = [parts[8 * i : 8 * i + 8, :] for i in range(parts.shape[0] // 8)]
    while len(tiles) > 1:
        tiles = [a + b for a, b in zip(tiles[::2], tiles[1::2])]
    total = tiles[0] + pltpu.roll(tiles[0], 4, 0)
    return total + pltpu.roll(total, 2, 0)


def middle_kernel(parts, out):
    total = sum_copies(parts)
    for i in range(out.shape[0] // 8):
        out[8 * i : 8 * i + 8, :] = total


def total_kernel(parts, out):
    total = sum_copies(parts)
    rows = jnp.where(row_of((BANDS, LANES)) < 8, total[0:1], total[1:2])
    own = (row_of((BANDS, LANES)) & 7) == lane_of((BANDS, LANES)) // BANDS
    fold = (row_of((LANES, BANDS)) & 15) == lane_of((LANES, BANDS))
    square = dot(jnp.where(own, rows, 0.0), fold.astype(jnp.float32), ((1,), (0,)))
    out[...] = square * (1.0 / (GX * GY * 1024))


def in_hbm(x):
    return pltpu.with_memory_space_constraint(x, pltpu.HBM)


def f32(*shape):
    return jax.ShapeDtypeStruct(shape, jnp.float32)


def params(mib=None):
    return pltpu.CompilerParams(vmem_limit_bytes=None if mib is None else mib << 20)


ATOM_TABLES = (CAP + GROUP, TILES * 8, LANES)


def atoms_call(held, offsets, beta, coupling):
    return pl.pallas_call(
        atoms_kernel,
        out_shape=(
            pltpu.VMEM((beta.shape[0], TILES * 8, LANES), jnp.float32),
            pltpu.VMEM(ATOM_TABLES, jnp.float32),
            pltpu.VMEM((LIST,), jnp.int32),
        ),
        in_specs=[VMEM] * 4,
        out_specs=(VMEM,) * 3,
        scratch_shapes=[
            pltpu.VMEM((BLOCKS, LANES), jnp.int32),
            pltpu.SMEM((BLOCKS, LANES), jnp.int32),
            pltpu.SMEM((3 * CAP + 1024,), jnp.int32),
            pltpu.SemaphoreType.DMA((2,)),
        ],
        compiler_params=params(20),
        cost_estimate=pl.CostEstimate(flops=10**8, bytes_accessed=10**7, transcendentals=0),
        name="atoms",
    )(held, offsets, beta, coupling)


def filter_call(held, low_in, high_in, sphere, rolled, atom_list):
    return pl.pallas_call(
        filter_kernel,
        out_shape=f32(BLOCKS, 4, 8, LANES),
        in_specs=[VMEM] * 6,
        out_specs=VMEM,
        scratch_shapes=[
            pltpu.VMEM((ROWS, LANES), jnp.float32),
            pltpu.VMEM((ROWS, LANES), jnp.float32),
            pltpu.VMEM((GX * GY, LANES), jnp.float32),
            pltpu.VMEM((2, 4 * GY, LANES), jnp.float32),
            pltpu.VMEM(ATOM_TABLES, jnp.float32),
            pltpu.VMEM((2 * CAP // GROUP, 8, LANES), jnp.float32),
            pltpu.VMEM((2 * CAP, LANES), jnp.float32),
            pltpu.VMEM((BLOCKS, LANES), jnp.int32),
            pltpu.SMEM((BLOCKS, LANES), jnp.int32),
            pltpu.SMEM((LIST,), jnp.int32),
            pltpu.SMEM((3 * CAP + 1024,), jnp.int32),
            pltpu.SemaphoreType.DMA((2,)),
        ],
        compiler_params=params(28),
        name="filter",
    )(held, low_in, high_in, sphere, rolled, atom_list)


def shards(wave, potential, positions, species, counts, offsets, beta, coupling):
    packed = pl.pallas_call(
        pack_kernel,
        out_shape=f32(BLOCKS, 9, 8, LANES),
        in_specs=[pl.BlockSpec(memory_space=pltpu.HBM)] * 5,
        out_specs=VMEM,
        scratch_shapes=[
            pltpu.VMEM(positions.shape, jnp.int32),
            pltpu.VMEM((1, SLOTS), jnp.int32),
            pltpu.VMEM((1, 1), jnp.int32),
            pltpu.VMEM(wave.shape, jnp.float32),
            pltpu.VMEM(potential.shape, jnp.float32),
            pltpu.VMEM((8, LANES), jnp.float32),
            pltpu.SemaphoreType.DMA((8,)),
        ],
        compiler_params=params(16),
        name="pack",
    )(in_hbm(positions), in_hbm(species[None]), counts[None], in_hbm(wave), in_hbm(potential))
    held = lax.all_to_all(packed, ("slab", "row"), split_axis=0, concat_axis=0, tiled=True)

    low_edge, high_edge = pl.pallas_call(
        edge_kernel,
        out_shape=(f32(HALO_ROWS, LANES), f32(HALO_ROWS, LANES)),
        in_specs=[VMEM],
        out_specs=(VMEM, VMEM),
        compiler_params=params(16),
        name="edges",
    )(held)

    order = [((h + 2 * pair + col) % 4) * 8 + col for pair in range(2) for col in range(8) for h in range(2)]
    chains = (order[:16], order[16:])
    up = [(a, b) for chain in chains for a, b in zip(chain[:-1], chain[1:])]
    down = [(b, a) for a, b in up]
    low_in = lax.ppermute(high_edge, ("slab", "col"), up)
    high_in = lax.ppermute(low_edge, ("slab", "col"), down)

    atoms = atoms_call(held, offsets.reshape(-1, offsets.shape[2]), beta, coupling[None])
    filtered = filter_call(held, low_in, high_in, *atoms)
    back = lax.all_to_all(filtered, ("slab", "row"), split_axis=0, concat_axis=0, tiled=True)
    result, partial = pl.pallas_call(
        unpack_kernel,
        out_shape=(f32(*wave.shape), f32(512, LANES)),
        in_specs=[VMEM],
        out_specs=(VMEM, VMEM),
        compiler_params=params(16),
        name="unpack",
    )(back)

    parts = lax.all_to_all(
        partial, ("slab", "row", "col"), split_axis=0, concat_axis=0, tiled=True
    )
    gram = pl.pallas_call(
        total_kernel,
        out_shape=f32(BANDS, BANDS),
        in_specs=[VMEM],
        out_specs=VMEM,
        name="total",
    )(parts)
    return result, gram


def solution(mesh):
    in_specs = (
        P(None, "slab", "row", "col"),
        P("slab", "row", "col"),
        P(None, ("slab", "row", "col")),
        P(("slab", "row", "col")),
        P(("slab", "row", "col")),
        P(),
        P(),
        P(),
    )
    out_specs = (P(None, "slab", "row", "col"), P())
    return jax.shard_map(shards, mesh=mesh, in_specs=in_specs, out_specs=out_specs, check_vma=False)
```

```python
import jax
import jax.numpy as jnp
from jax import lax
from jax.experimental import pallas as pl
from jax.experimental.pallas import tpu as pltpu
from jax.sharding import PartitionSpec as P

stencil_weights = (
    -5369.0 / 1800.0,
    12.0 / 7.0,
    -15.0 / 56.0,
    10.0 / 189.0,
    -1.0 / 112.0,
    2.0 / 1925.0,
    -1.0 / 16632.0,
)
lower_edge = 3.0
upper_edge = 17.0
centre = 0.5 * (upper_edge + lower_edge)
half_width = 0.5 * (upper_edge - lower_edge)

BANDS = 16
GX, GY, LANES = 32, 64, 128
PX, PY = 6, 8
PITCH = GY + 2 * PY
ROWS = (GX + 2 * PX) * PITCH
TILES = 11
BLOCKS = 32
DEVICES = 256
SLOTS = 8
GROUP = 8
UNROLL = 4
CAP = BLOCKS * SLOTS
LIST = 1024
HALO_ROWS = BLOCKS * 33
VMEM = pl.BlockSpec(memory_space=pltpu.VMEM)
HIGHEST = lax.Precision.HIGHEST


def lane_of(shape):
    return lax.broadcasted_iota(jnp.int32, shape, len(shape) - 1)


def row_of(shape):
    return lax.broadcasted_iota(jnp.int32, shape, len(shape) - 2)


def pack_kernel(
    positions_in,
    species_in,
    counts_in,
    wave_in,
    potential_in,
    out,
    positions,
    species,
    counts,
    wave,
    potential,
    info,
    sems,
):
    copies = [
        pltpu.make_async_copy(potential_in, potential, sems.at[0]),
        pltpu.make_async_copy(positions_in, positions, sems.at[1]),
        pltpu.make_async_copy(species_in, species, sems.at[2]),
        pltpu.make_async_copy(counts_in, counts, sems.at[3]),
    ]
    for piece in range(4):
        bands = pl.ds(4 * piece, 4)
        copies.append(
            pltpu.make_async_copy(wave_in.at[bands], wave.at[bands], sems.at[4 + piece])
        )
    for copy in copies:
        copy.start()
    for copy in copies[:4]:
        copy.wait()
    col = lax.axis_index("col")
    low = lane_of((8, LANES)) < 64
    live = jnp.where(lane_of((1, SLOTS)) < counts[...], 1, 0)
    rows = [positions[k : k + 1, :] for k in range(3)] + [species[...], live]
    info[...] = jnp.zeros((8, LANES), jnp.float32)
    for k, values in enumerate(rows):
        info[0:1, SLOTS * k : SLOTS * (k + 1)] = values.astype(jnp.float32)

    def halves(tile, other):
        return (
            jnp.where(low, tile, pltpu.roll(other, 64, 1)),
            jnp.where(low, pltpu.roll(tile, 64, 1), other),
        )

    fixed = [halves(potential[k], potential[k + 4]) for k in range(4)]
    for pair in range(2):
        slabs = [lax.rem(2 * pair + h + col, 4) for h in range(2)]
        for r in range(8):
            if r % 4 == 0:
                copies[4 + 2 * pair + r // 4].wait()
            band = pair * 8 + r
            for k in range(4):
                parts = halves(wave[band, k], wave[band, k + 4])
                for h in range(2):
                    dest = slabs[h] * 8 + r
                    out[dest, k] = parts[h]
                    out[dest, 4 + k] = fixed[k][h]
            for h in range(2):
                out[slabs[h] * 8 + r, 8] = info[...]


def edge_kernel(held, low_out, high_out):
    even = (lane_of((8, LANES)) & 32) == 0

    def one(i, carry):
        for d in [i * UNROLL + k for k in range(UNROLL)]:
            for tile in range(4):
                first = held[d, 2 * tile]
                second = pltpu.roll(held[d, 2 * tile + 1], 32, 1)
                at = pl.multiple_of(d * 32, 32) + tile * 8
                low_out[pl.ds(at, 8), :] = jnp.where(even, first, second)
                high_out[pl.ds(at, 8), :] = jnp.where(even, second, first)
        return carry

    lax.fori_loop(0, BLOCKS // UNROLL, one, 0)
    rows = held[:, 8, 0, :]
    low_out[BLOCKS * 32 :, :] = rows
    high_out[BLOCKS * 32 :, :] = rows


def fill_sphere(offsets, beta, coupling, out):
    points = beta.shape[1]
    for kind in range(beta.shape[0]):
        dx = offsets[3 * kind : 3 * kind + 1, :]
        dy = offsets[3 * kind + 1 : 3 * kind + 2, :]
        dz = offsets[3 * kind + 2 : 3 * kind + 3, :]
        row = 16 + (dx + 3) * 8 + dy + 4
        row = jnp.where(jnp.abs(dx) == 4, jnp.where(dx > 0, 8, 0) + dy + 3, row)
        row = jnp.where(dy == 4, 72 + dx + 3, row)
        row = jnp.where(jnp.abs(dy) == 5, jnp.where(dy > 0, 81, 80), row)
        row = jnp.where(jnp.abs(dx) == 5, jnp.where(dx > 0, 83, 82), row)
        left = (row_of((TILES * 8, points)) == row).astype(jnp.float32)
        values = beta[kind : kind + 1, :] * jnp.sqrt(coupling[0:1, kind : kind + 1])
        right = jnp.where(row_of((LANES, points)) == dz + 5, values, 0.0)
        out[kind] = lax.dot_general(
            left,
            right,
            (((1,), (1,)), ((), ())),
            precision=HIGHEST,
            preferred_element_type=jnp.float32,
        )


def tile_refs(ref, base):
    yield ref.at[pl.ds(base - 4 * PITCH - 3, 8), :]
    yield ref.at[pl.ds(base + 4 * PITCH - 3, 8), :]
    for dx in range(-3, 4):
        yield ref.at[pl.ds(base + dx * PITCH - 4, 8), :]
    yield ref.at[pl.ds(base - 3 * PITCH + 4, 8, stride=PITCH), :]
    yield ref.at[pl.ds(base - 5, 2, stride=10), :]
    yield ref.at[pl.ds(base - 5 * PITCH, 2, stride=10 * PITCH), :]


TILE_ROWS = (8,) * 10 + (2, 2)
TILE_AT = tuple(8 * t for t in range(11)) + (82,)


def place_along_z():
    slab, col = lax.axis_index("slab"), lax.axis_index("col")
    half = lax.rem(slab + 4 - lax.rem(col, 4), 4) % 2
    return half, col * 2 + half


def atom_words(rows, depth):
    rows = rows.astype(jnp.int32)
    x, y, along, kind, live = (
        rows if k == 0 else pltpu.roll(rows, LANES - SLOTS * k, 1) for k in range(5)
    )
    along = along - (depth * 64 - 32)
    code = jnp.where((along >= 7) & (along < 121), 2, 3)
    code = code - jnp.where((along >= 17) & (along < 111), 1, 0)
    code = code - jnp.where((along >= 27) & (along < 101), 1, 0)
    code = jnp.where(live > 0, code, 3)
    turn = (along - 37) & (LANES - 1)
    spot = (x + PX) * PITCH + y + PY
    return jnp.where(code < 3, (spot * 4 + kind) * 512 + turn * 4 + code, 3)


def list_rows(table, listed, first_row, count, lengths):
    words = [table[first_row + k, slot] for k in range(count) for slot in range(SLOTS)]
    for word in words:
        code = word & 3
        shift = code * 10
        listed[(lax.shift_right_logical(lengths, shift) & 1023) + code * CAP] = word
        lengths = lengths + lax.shift_left(jnp.int32(1), shift)
    return lengths


def join_lists(listed, lengths):
    n0, n1, n2 = lengths & 1023, (lengths >> 10) & 1023, (lengths >> 20) & 1023

    def move_second(i, carry):
        listed[n0 + i] = listed[CAP + i]
        return carry

    def move_third(i, carry):
        listed[n0 + n1 + i] = listed[2 * CAP + i]
        return carry

    lax.fori_loop(0, n1, move_second, 0)
    lax.fori_loop(0, n2, move_third, 0)
    for i in range(GROUP - 1):
        listed[n0 + n1 + n2 + i] = (PX * PITCH + PY) << 11
    return n0 + n1 + n2, n0 + n1, n0


def lane_mask(depth):
    lanes = lane_of((1, LANES))
    outside = ((lanes >= 96) & (depth == 0)) | ((lanes >= 64) & (lanes < 96) & (depth == 15))
    return jnp.where(outside, 0.0, 1.0)


def turn_sphere(sphere, word, mask, rolled, j):
    kind = (word >> 9) & 3
    turn = (word >> 2) & 127
    for t in range(TILES):
        rows = slice(8 * t, 8 * t + 8)
        rolled[j, rows, :] = pltpu.roll(sphere[kind, rows, :], turn, 1) * mask


def atoms_kernel(
    held, offsets, beta, coupling, sphere, rolled, list_out, table_v, table, listed, sems
):
    half, depth = place_along_z()
    table_v[...] = atom_words(held[:, 8, 0, :], depth)
    copy = pltpu.make_async_copy(table_v, table, sems.at[0])
    copy.start()
    fill_sphere(offsets, beta, coupling, sphere)
    copy.wait()

    def build(i, lengths):
        return list_rows(table, listed, 4 * i, 4, lengths)

    lengths = lax.fori_loop(0, BLOCKS // 4, build, jnp.int32(0))
    counts = join_lists(listed, lengths)
    for k in range(3):
        listed[LIST - 3 + k] = counts[k]
    copy = pltpu.make_async_copy(listed.at[pl.ds(0, LIST)], list_out, sems.at[1])
    copy.start()
    mask = lane_mask(depth)

    def turn_group(i, carry):
        for j in [i * 4 + k for k in range(4)]:
            turn_sphere(sphere, listed[j], mask, rolled, j)
        return carry

    lax.fori_loop(0, (counts[0] + 3) // 4, turn_group, 0)
    copy.wait()


def filter_kernel(
    held,
    low_in,
    high_in,
    sphere,
    rolled,
    list_in,
    out,
    buf_a,
    buf_b,
    pot,
    parts,
    outer_rolled,
    acc,
    total,
    table_v,
    table,
    listed,
    outer_listed,
    sems,
):
    half, depth = place_along_z()
    lane8, row8 = lane_of((8, LANES)), row_of((8, LANES))

    outer = jnp.where(half == 0, low_in[BLOCKS * 32 :, :], high_in[BLOCKS * 32 :, :])
    table_v[...] = atom_words(outer, depth)
    copies = [
        pltpu.make_async_copy(table_v, table, sems.at[0]),
        pltpu.make_async_copy(list_in, listed, sems.at[1]),
    ]
    for copy in copies:
        copy.start()

    edge = PX * PITCH

    def clear_edges(target):
        target[0:edge, :] = jnp.zeros((edge, LANES), jnp.float32)
        target[ROWS - edge :, :] = jnp.zeros((edge, LANES), jnp.float32)

        for x in range(PX, PX + GX):
            at = x * PITCH
            target[at : at + PY, :] = jnp.zeros((PY, LANES), jnp.float32)
            target[at + PY + GY : at + PITCH, :] = jnp.zeros((PY, LANES), jnp.float32)

    clear_edges(buf_a)
    for copy in copies:
        copy.wait()

    low = lane8 < 64
    even = (lane8 & 32) == 0

    def gather_block(d):
        s, r = d // 8, lax.rem(d, 8)
        for field in range(2):
            for pair in range(2):
                at = pl.multiple_of(d * 32, 32) + field * 16 + pair * 8
                above = high_in[pl.ds(at, 8), :]
                below = low_in[pl.ds(at, 8), :]
                evens = jnp.where(even, above, below)
                odds = jnp.where(even, below, above)
                turned = (
                    pltpu.roll(evens, 64, 1),
                    pltpu.roll(odds, 32, 1),
                    evens,
                    pltpu.roll(odds, 96, 1),
                )
                for m in range(2):
                    own = held[d, field * 4 + 2 * pair + m]
                    for high in range(2):
                        x = 4 * high + 2 * pair + m
                        mid = pltpu.roll(own, 64, 1) if high else own
                        tile = jnp.where(low, mid, turned[2 * high + m])
                        if field == 0:
                            to = pl.multiple_of((s * 8 + x + PX) * PITCH + PY + r * 8, 8)
                            buf_a[pl.ds(to, 8), :] = tile
                        else:
                            to = pl.multiple_of((s * 8 + x) * GY + r * 8, 8)
                            pot[pl.ds(to, 8), :] = tile - (centre + 1.5 * stencil_weights[0])

    def blocks(i, lengths):
        for k in range(UNROLL):
            gather_block(i * UNROLL + k)
        return list_rows(table, outer_listed, UNROLL * i, UNROLL, lengths)

    lengths = lax.fori_loop(0, BLOCKS // UNROLL, blocks, jnp.int32(0))
    outer_counts = join_lists(outer_listed, lengths)
    own_counts = [listed[LIST - 3 + k] for k in range(3)]
    own_groups = (own_counts[0] + GROUP - 1) // GROUP

    apart = jnp.abs(lane_of((LANES, LANES)) - row_of((LANES, LANES)))
    apart = jnp.minimum(apart, LANES - apart)
    band = jnp.zeros((LANES, LANES), jnp.float32)
    for reach in range(1, 7):
        band = jnp.where(apart == reach, -0.5 * stencil_weights[reach], band)
    z_high = band.astype(jnp.bfloat16)
    z_low = (band - z_high.astype(jnp.float32)).astype(jnp.bfloat16)
    z_band = jnp.concatenate(
        [
            jnp.concatenate([z_high, z_low], axis=1),
            jnp.concatenate([z_high, jnp.zeros_like(z_low)], axis=1),
        ],
        axis=0,
    )
    planes = 4
    mask = lane_mask(depth)

    def products(source, g, slot):
        first = g * (planes * PITCH) + PX * PITCH + PY
        field = jnp.concatenate(
            [source[pl.ds(first + x * PITCH, GY), :] for x in range(planes)], axis=0
        )
        high = field.astype(jnp.bfloat16)
        small = (field - high.astype(jnp.float32)).astype(jnp.bfloat16)
        both = jnp.concatenate([high, small], axis=1)
        along_z = jnp.dot(both, z_band, preferred_element_type=jnp.float32)
        parts[slot] = along_z[:, :LANES] + along_z[:, LANES:]

    def local_part(source, target, scale, subtract):
        factor = mask * scale

        def one(g, carry, more=True):
            slot = g & 1
            first = g * (planes * PITCH) + PX * PITCH + PY
            for t in range(GY // 8):
                line = [
                    source[pl.ds(first + (x - PX) * PITCH + 8 * t, 8), :]
                    for x in range(planes + 2 * PX)
                ]
                for x in range(planes):
                    at = x * GY + 8 * t
                    own_at = g * (planes * GY) + at
                    to = first + x * PITCH + 8 * t
                    result = parts[slot, at : at + 8, :] + pot[pl.ds(own_at, 8), :] * line[x + PX]
                    for reach in range(1, 7):
                        near = line[x + PX - reach] + line[x + PX + reach]
                        near += source[pl.ds(to - reach, 8), :] + source[pl.ds(to + reach, 8), :]
                        result += (-0.5 * stencil_weights[reach]) * near
                    result = result * factor
                    if subtract:
                        result -= target[pl.ds(to, 8), :]
                    target[pl.ds(to, 8), :] = result
            if more:
                products(source, g + 1, 1 - slot)
            return carry

        products(source, 0, 0)
        for g in range(GX // planes):
            one(g, 0, g < GX // planes - 1)

    def gather_atoms(source, atoms, tables, count, first_group, turn):
        def one(i, carry):
            sums = []
            for j in [i * GROUP + k for k in range(GROUP)]:
                word = atoms[j]
                if turn:
                    turn_sphere(sphere, word, mask, tables, j)
                terms = []
                for t, ref in enumerate(tile_refs(source, word >> 11)):
                    terms.append(ref[...] * tables[j, TILE_AT[t] : TILE_AT[t] + TILE_ROWS[t], :])
                small = terms[10] + terms[11]
                terms[10:] = [jnp.concatenate([small, jnp.zeros((6, LANES), jnp.float32)], axis=0)]
                while len(terms) > 1:
                    rest = terms[len(terms) // 2 * 2 :]
                    terms = [a + b for a, b in zip(terms[::2], terms[1::2])] + rest
                sums.append(terms[0])
            for width in (1, 2, 4):
                keep = (row8 & width) == 0
                sums = [
                    jnp.where(keep, a, b) + pltpu.roll(jnp.where(keep, b, a), width, 0)
                    for a, b in zip(sums[::2], sums[1::2])
                ]
            acc[first_group + i] = sums[0]
            return carry

        lax.fori_loop(0, (count + GROUP - 1) // GROUP, one, 0)

    def sum_atoms(count, scale):
        size = 8 * GROUP

        def one(i, carry):
            at = pl.multiple_of(i * size, size)
            part = acc[pl.ds(pl.multiple_of(i * 8, 8), 8)].reshape(size, LANES)
            part = jnp.sum(part, axis=1, keepdims=True) * scale
            total[pl.ds(at, size), :] = jnp.broadcast_to(part, (size, LANES))
            return carry

        lax.fori_loop(0, (count + size - 1) // size, one, 0)

    def spread_atoms(target, atoms, tables, count, first):
        def one(j, carry):
            q = total[pl.ds(first + j, 1), :]
            refs = list(tile_refs(target, atoms[j] >> 11))
            values = []
            for t, ref in enumerate(refs):
                values.append(ref[...] + q * tables[j, TILE_AT[t] : TILE_AT[t] + TILE_ROWS[t], :])
            for ref, value in zip(refs, values):
                ref[...] = value
            return carry

        lax.fori_loop(0, count, one, 0)

    def step(source, target, scale, subtract, which):
        own, outer = own_counts[which], outer_counts[which]
        gather_atoms(source, listed, rolled, own, 0, False)
        gather_atoms(source, outer_listed, outer_rolled, outer, own_groups, which == 0)
        sum_atoms(own_groups * GROUP + outer, scale)
        local_part(source, target, scale, subtract)
        spread_atoms(target, listed, rolled, own, 0)
        spread_atoms(target, outer_listed, outer_rolled, outer, own_groups * GROUP)

    step(buf_a, buf_b, 1.0 / half_width, False, 0)
    clear_edges(buf_b)
    step(buf_b, buf_a, 2.0 / half_width, True, 1)
    clear_edges(buf_a)
    step(buf_a, buf_b, 2.0 / half_width, True, 2)

    def send_blocks(i, carry):
        for d in [i * UNROLL + k for k in range(UNROLL)]:
            s, r = d // 8, lax.rem(d, 8)
            for k in range(4):
                at = pl.multiple_of((s * 8 + k + PX) * PITCH + PY + r * 8, 8)
                first = buf_b[pl.ds(at, 8), :]
                second = buf_b[pl.ds(at + 4 * PITCH, 8), :]
                out[d, k] = jnp.where(low, first, pltpu.roll(second, 64, 1))
        return carry

    lax.fori_loop(0, BLOCKS // UNROLL, send_blocks, 0)


def dot(a, b, dims):
    return lax.dot_general(
        a, b, (dims, ((), ())), precision=HIGHEST, preferred_element_type=jnp.float32
    )


def unpack_kernel(held, out, gram):
    col = lax.axis_index("col")
    low = lane_of((8, LANES)) < 64
    for pair in range(2):
        slabs = [lax.rem(2 * pair + h + col, 4) for h in range(2)]

        def one(i, carry):
            for r in [i * UNROLL + k for k in range(UNROLL)]:
                for k in range(4):
                    first = held[slabs[0] * 8 + r, k]
                    second = held[slabs[1] * 8 + r, k]
                    out[pair * 8 + r, k] = jnp.where(low, first, pltpu.roll(second, 64, 1))
                    out[pair * 8 + r, k + 4] = jnp.where(low, pltpu.roll(first, 64, 1), second)
            return carry

        lax.fori_loop(0, 8 // UNROLL, one, 0)

    size = BANDS * 8
    products = jnp.zeros((size, size), jnp.float32)
    for x in range(8):
        plane = out[:, x].reshape(size, LANES)
        high = plane.astype(jnp.bfloat16)
        small = (plane - high.astype(jnp.float32)).astype(jnp.bfloat16)
        products += lax.dot_general(
            jnp.concatenate([high, high, small], axis=1),
            jnp.concatenate([high, small, high], axis=1),
            (((1,), (1,)), ((), ())),
            preferred_element_type=jnp.float32,
        )
    row, lane = row_of((size, size)), lane_of((size, size))
    products = jnp.where((row & 7) == (lane & 7), products, 0.0)
    rows = jnp.sum(products.reshape(BANDS, 8, LANES), axis=1)
    for width in (1, 2, 4):
        rows = rows + pltpu.roll(rows, LANES - width, 1)
    rows = jnp.where((lane_of((BANDS, LANES)) & 7) == 0, rows, 0.0)
    both = [
        jnp.sum(
            pltpu.roll(rows[8 * k : 8 * k + 8], 0, 1, stride=1, stride_axis=0),
            axis=0,
            keepdims=True,
        )
        for k in range(2)
    ]
    tile = jnp.concatenate(both * 4, axis=0)
    for i in range(gram.shape[0] // 8):
        gram[8 * i : 8 * i + 8, :] = tile


def sum_copies(parts):
    tiles = [parts[8 * i : 8 * i + 8, :] for i in range(parts.shape[0] // 8)]
    while len(tiles) > 1:
        tiles = [a + b for a, b in zip(tiles[::2], tiles[1::2])]
    total = tiles[0] + pltpu.roll(tiles[0], 4, 0)
    return total + pltpu.roll(total, 2, 0)


def total_kernel(parts, out):
    total = sum_copies(parts)
    total = total * (1.0 / (GX * GY * 1024))
    row, lane = row_of((BANDS, LANES)), lane_of((BANDS, LANES))
    rows = jnp.where(row < 8, total[0:1], total[1:2])
    rows = jnp.where((row & 7) == (lane & 7), rows, 0.0)
    fold = row_of((LANES, BANDS)) // 8 == lane_of((LANES, BANDS))
    out[...] = dot(rows, fold.astype(jnp.float32), ((1,), (0,)))


def in_hbm(x):
    return pltpu.with_memory_space_constraint(x, pltpu.HBM)


def f32(*shape):
    return jax.ShapeDtypeStruct(shape, jnp.float32)


def params(mib=None):
    return pltpu.CompilerParams(vmem_limit_bytes=None if mib is None else mib << 20)


ATOM_TABLES = (CAP + GROUP, TILES * 8, LANES)


def atoms_call(held, offsets, beta, coupling):
    return pl.pallas_call(
        atoms_kernel,
        out_shape=(
            pltpu.VMEM((beta.shape[0], TILES * 8, LANES), jnp.float32),
            pltpu.VMEM(ATOM_TABLES, jnp.float32),
            pltpu.VMEM((LIST,), jnp.int32),
        ),
        in_specs=[VMEM] * 4,
        out_specs=(VMEM,) * 3,
        scratch_shapes=[
            pltpu.VMEM((BLOCKS, LANES), jnp.int32),
            pltpu.SMEM((BLOCKS, LANES), jnp.int32),
            pltpu.SMEM((3 * CAP + 1024,), jnp.int32),
            pltpu.SemaphoreType.DMA((2,)),
        ],
        compiler_params=params(20),
        cost_estimate=pl.CostEstimate(flops=10**8, bytes_accessed=10**7, transcendentals=0),
        name="atoms",
    )(held, offsets, beta, coupling)


def filter_call(held, low_in, high_in, sphere, rolled, atom_list):
    return pl.pallas_call(
        filter_kernel,
        out_shape=f32(BLOCKS, 4, 8, LANES),
        in_specs=[VMEM] * 6,
        out_specs=VMEM,
        scratch_shapes=[
            pltpu.VMEM((ROWS, LANES), jnp.float32),
            pltpu.VMEM((ROWS, LANES), jnp.float32),
            pltpu.VMEM((GX * GY, LANES), jnp.float32),
            pltpu.VMEM((2, 4 * GY, LANES), jnp.float32),
            pltpu.VMEM(ATOM_TABLES, jnp.float32),
            pltpu.VMEM((2 * CAP // GROUP, 8, LANES), jnp.float32),
            pltpu.VMEM((2 * CAP, LANES), jnp.float32),
            pltpu.VMEM((BLOCKS, LANES), jnp.int32),
            pltpu.SMEM((BLOCKS, LANES), jnp.int32),
            pltpu.SMEM((LIST,), jnp.int32),
            pltpu.SMEM((3 * CAP + 1024,), jnp.int32),
            pltpu.SemaphoreType.DMA((2,)),
        ],
        compiler_params=params(28),
        name="filter",
    )(held, low_in, high_in, sphere, rolled, atom_list)


def unpack_call(back):
    return pl.pallas_call(
        unpack_kernel,
        out_shape=(f32(BANDS, 8, 8, LANES), f32(2 * DEVICES, LANES)),
        in_specs=[VMEM],
        out_specs=(VMEM, VMEM),
        compiler_params=params(16),
        name="unpack",
    )(back)


def total_call(parts):
    return pl.pallas_call(
        total_kernel,
        out_shape=f32(BANDS, BANDS),
        in_specs=[VMEM],
        out_specs=VMEM,
        name="total",
    )(parts)


def shards(wave, potential, positions, species, counts, offsets, beta, coupling):
    packed = pl.pallas_call(
        pack_kernel,
        out_shape=f32(BLOCKS, 9, 8, LANES),
        in_specs=[pl.BlockSpec(memory_space=pltpu.HBM)] * 5,
        out_specs=VMEM,
        scratch_shapes=[
            pltpu.VMEM(positions.shape, jnp.int32),
            pltpu.VMEM((1, SLOTS), jnp.int32),
            pltpu.VMEM((1, 1), jnp.int32),
            pltpu.VMEM(wave.shape, jnp.float32),
            pltpu.VMEM(potential.shape, jnp.float32),
            pltpu.VMEM((8, LANES), jnp.float32),
            pltpu.SemaphoreType.DMA((8,)),
        ],
        compiler_params=params(16),
        name="pack",
    )(in_hbm(positions), in_hbm(species[None]), counts[None], in_hbm(wave), in_hbm(potential))
    held = lax.all_to_all(packed, ("slab", "row"), split_axis=0, concat_axis=0, tiled=True)

    low_edge, high_edge = pl.pallas_call(
        edge_kernel,
        out_shape=(f32(HALO_ROWS, LANES), f32(HALO_ROWS, LANES)),
        in_specs=[VMEM],
        out_specs=(VMEM, VMEM),
        compiler_params=params(16),
        name="edges",
    )(held)

    order = [((h + 2 * pair + col) % 4) * 8 + col for pair in range(2) for col in range(8) for h in range(2)]
    chains = (order[:16], order[16:])
    up = [(a, b) for chain in chains for a, b in zip(chain[:-1], chain[1:])]
    down = [(b, a) for a, b in up]
    low_in = lax.ppermute(high_edge, ("slab", "col"), up)
    high_in = lax.ppermute(low_edge, ("slab", "col"), down)

    atoms = atoms_call(held, offsets.reshape(-1, offsets.shape[2]), beta, coupling[None])
    filtered = filter_call(held, low_in, high_in, *atoms)
    back = lax.all_to_all(filtered, ("slab", "row"), split_axis=0, concat_axis=0, tiled=True)
    result, partial = unpack_call(back)
    parts = lax.all_to_all(
        partial, ("slab", "row", "col"), split_axis=0, concat_axis=0, tiled=True
    )
    gram = total_call(parts)
    return result, gram


def solution(mesh):
    in_specs = (
        P(None, "slab", "row", "col"),
        P("slab", "row", "col"),
        P(None, ("slab", "row", "col")),
        P(("slab", "row", "col")),
        P(("slab", "row", "col")),
        P(),
        P(),
        P(),
    )
    out_specs = (P(None, "slab", "row", "col"), P())
    return jax.shard_map(shards, mesh=mesh, in_specs=in_specs, out_specs=out_specs, check_vma=False)
```
